512 devices in a mesh: mu: 128 (over z, y, core), pa: 4 (over x).
Axes of the slice: x: 4, y: 8, z: 8, core: 2. Of those that a mesh axis runs over, the one named last changes fastest.
Arguments:
- three_center: bfloat16 [640, 64, 16384], P('mu', None, 'pa'), may hold values from -6 to 6
- pair_mu: int32 [128, 5], P('mu'), may hold values from 0 to 47
- pair_site: int32 [128, 5, 1], P('mu'), may hold values from 0 to 3; in each aligned block of 5 rows (0 to 4, 5 to 9, ..., all dimensions but the last counted through in order) at most 2 rows name the same one
- pair_pos: int32 [128, 5], P('mu'), may hold values from 0 to 11
- coeff: bfloat16 [3072, 32], replicated, may hold values from -0.21875 to 0.21875
- fitting: bfloat16 [48, 256, 256], P(None, 'pa'), as said below
Outputs:
- gfit: bfloat16 [128, 12, 1, 16384], P('mu', None, None, 'pa')
The draws below stay inside these ranges and needn't reach their ends.
Inputs may be any that keep to these rules, and one draw needn't show every extreme that they name: `pair_site`: of the 5 pairs listed for one index of mu, at most 2 name the same site, and 2 is reached. Every fitting[b] is a symmetric matrix.
All inputs are finite; a program needn't handle non-finite values.
Results may differ from the reference program's by a relative error of at most 0.0058.
Values may be sent and summed in bfloat16 or wider, within the bound.
No kernel may reach another device: no remote copies, remote signals or barrier semaphores. Data moves between devices by JAX's collectives and lax.ppermute only.
A program may use at most 64 MiB of HBM per device.

```python
import math
import jax
import jax.numpy as jnp
import numpy as np
from jax import lax

BS = 64
PL = 256
PLS = 64
SITES = 4
NU_SITE = 12
NBO = 48
NAO = 3072
NT = 5
CAP = 2
IG_SZ = 1
NOB = 32
N_MU = 128
N_PA = 4


def draw_fitting(key, part):
    shape = (NBO, PL, PL)
    base = jax.random.normal(key, shape, jnp.float32)
    symmetric = (base + jnp.swapaxes(base, 1, 2)) * 0.5 ** 0.5 * PL ** (-0.5)
    return symmetric.astype(jnp.bfloat16)


def set_ends(drawn, key, least, largest):
    longest = drawn.shape.index(max(drawn.shape))
    spots = []
    for shift in (0, 1):
        where = [jax.random.randint(jax.random.fold_in(key, axis), (), 0, length) for axis, length in enumerate(drawn.shape)]
        where[longest] = (where[longest] + shift) % drawn.shape[longest]
        spots.append(tuple(where))
    return drawn.at[spots[0]].set(least).at[spots[1]].set(largest)


def steps_of(key, shape, pieces, low, top_value):
    level = 1.0
    for position, blocks in pieces:
        steps = jax.random.uniform(jax.random.fold_in(jax.random.fold_in(key, 6), position), (blocks,), jnp.float32, low / len(pieces), top_value / len(pieces))
        level = level * jnp.repeat(jnp.exp(steps), shape[position] // blocks).reshape((-1,) + (1,) * (len(shape) - 1 - position))
    return level


def routed_block(stream_key, own, number, rows, count, top, limit, slope):
    order = jax.random.permutation(stream_key, count)
    heavy_load, common = load_shares(count, rows * top, limit, slope, True), load_shares(count, rows * top, limit, slope, False)
    places = jnp.arange(count)

    def named(tallies, turn):
        used = int((tallies > 0).sum())
        fixed = max(1, used // 4)
        shifted = fixed + (places - fixed + turn * (used - fixed)) % max(1, count - fixed)
        return jnp.zeros((count,), jnp.int32).at[order[jnp.where(places < fixed, places, shifted)]].set(jnp.asarray(tallies, jnp.int32))

    tallies = jnp.where(number % 4 == 0, named(heavy_load, number // 4), named(common, number - number // 4 - 1))
    mixed = jax.random.permutation(jax.random.fold_in(own, 3), count)
    source_of, sink = mixed[0:count // 2 * 2:2], mixed[1:count // 2 * 2:2]
    slack = jnp.minimum(tallies[source_of] - 1, limit - tallies[sink]) // 2
    slack = jnp.where((source_of == order[0]) | (sink == order[0]) | (tallies[sink] == 0), 0, jnp.maximum(slack, 0))
    shifted = jax.random.randint(jax.random.fold_in(own, 4), (count // 2,), 0, 1 << 20) % (slack + 1)
    tallies = tallies.at[source_of].add(-shifted).at[sink].add(shifted)
    items = jnp.searchsorted(jnp.cumsum(tallies), jnp.arange(rows * top), side="right").astype(jnp.int32)
    table = items.reshape(top, rows).T
    table = table[jax.random.permutation(jax.random.fold_in(own, 1), rows)]
    turn = jax.random.randint(jax.random.fold_in(own, 2), (rows, 1), 0, top)
    return jnp.take_along_axis(table, (jnp.arange(top)[None, :] + turn) % top, axis=1)


def load_shares(count, total, reach, skew, full):
    loads = [(1 << 20) // math.isqrt(standing ** skew) + 1 for standing in range(1, count + 1)]
    largest = reach if full else min(reach, max(-(-total // count), total * loads[0] // sum(loads)))
    least = 1 if total - largest >= count - 1 else 0
    given, spare = [largest] + [least] * (count - 1), total - largest - least * (count - 1)
    while spare > 0:
        candidates = [i for i in range(1, count) if given[i] < largest] or [i for i in range(1, count) if given[i] < reach]
        whole, remaining = sum([loads[i] for i in candidates]), spare
        for i in candidates:
            extra = min(reach - given[i], max(1, remaining * loads[i] // whole), spare)
            given[i] = given[i] + extra
            spare = spare - extra
    return np.array(given)


def centred(rng, extent, width, most, shards=(), held_as=jnp.bfloat16):
    result = width * jax.random.normal(rng, extent, jnp.float32)
    if shards:
        result = result * steps_of(rng, extent, shards, -0.22, 0.18)
    return jnp.clip(result, -most, most).astype(held_as)


def setup_inputs(seed: int = 0) -> dict:
    arg_keys = jax.random.split(jax.random.key(seed), 7)
    three_center = centred(arg_keys[0], (N_MU * NT, BS, N_PA * BS * PLS), 1.0, 6.0, ((0, 128), (2, 4)))
    pair_mu = set_ends(jax.random.randint(arg_keys[1], (N_MU, NT), 0, NBO), jax.random.fold_in(arg_keys[1], 1), 0, NBO - 1).astype(jnp.int32)
    pair_site_keys = jax.random.split(jax.random.fold_in(arg_keys[2], 1), N_MU * NT // NT)
    pair_site_turns = jax.random.permutation(jax.random.fold_in(arg_keys[2], 3), N_MU * NT // NT)
    pair_site = jax.vmap(lambda own, number: routed_block(jax.random.fold_in(arg_keys[2], 2), own, number, NT, SITES, 1, CAP, 2))(pair_site_keys, pair_site_turns).reshape((N_MU, NT, 1))
    pair_pos = set_ends(jax.random.randint(arg_keys[3], (N_MU, NT), 0, NU_SITE), jax.random.fold_in(arg_keys[3], 1), 0, NU_SITE - 1).astype(jnp.int32)
    coeff = centred(arg_keys[4], (NAO, NOB), (BS * NU_SITE) ** -0.5, 0.21875)
    fitting = draw_fitting(jax.random.fold_in(arg_keys[6], 71), 0)
    return {"three_center": three_center, "pair_mu": pair_mu, "pair_site": pair_site, "pair_pos": pair_pos, "coeff": coeff, "fitting": fitting}


def reference(three_center, pair_mu, pair_site, pair_pos, coeff, fitting):
    groups = N_MU // SITES
    full_width = N_PA * BS * PLS
    mu_blocks = coeff.reshape(NBO, BS, NOB)
    mu_list = pair_mu.reshape(-1).astype(jnp.int32)
    site_list = pair_site.reshape(-1).astype(jnp.int32)
    pos_list = pair_pos.reshape(-1).astype(jnp.int32)

    def add_pair(fitted, pair_index):
        block_rows = lax.dynamic_index_in_dim(mu_blocks, mu_list[pair_index], 0, keepdims=False)
        slab_rows = lax.dynamic_index_in_dim(three_center, pair_index, 0, keepdims=False)
        piece_sum = jnp.dot(block_rows.T, slab_rows, preferred_element_type=jnp.float32).astype(jnp.bfloat16)
        piece_sum = lax.optimization_barrier(piece_sum).astype(jnp.float32).reshape(groups, IG_SZ, full_width)
        updated = fitted.at[:, site_list[pair_index], pos_list[pair_index]].add(piece_sum)
        return updated, None

    initial = jnp.zeros((groups, SITES, NU_SITE, IG_SZ, full_width), jnp.float32)
    fitted, unused_out = lax.scan(add_pair, initial, jnp.arange(N_MU * NT, dtype=jnp.int32))
    rounded = fitted.astype(jnp.bfloat16).reshape(N_MU, NU_SITE, IG_SZ, N_PA, BS, PLS)
    arranged = jnp.transpose(rounded, (0, 1, 2, 4, 3, 5)).reshape(N_MU, NU_SITE, IG_SZ, BS, PL)
    site_weights = fitting.reshape(SITES, NU_SITE, PL, PL)

    def one_owner(owner_index):
        rows_here = lax.dynamic_index_in_dim(arranged, owner_index, 0, keepdims=False).astype(jnp.float32)
        weights = lax.dynamic_index_in_dim(site_weights, owner_index % SITES, 0, keepdims=False).astype(jnp.float32)
        product = jnp.einsum("kinp,kqp->kinq", rows_here, weights)
        product = product.reshape(NU_SITE, IG_SZ, BS, N_PA, PLS)
        product = jnp.transpose(product, (0, 1, 3, 2, 4)).reshape(NU_SITE, IG_SZ, full_width)
        return product.astype(jnp.bfloat16)

    return lax.map(one_owner, jnp.arange(N_MU, dtype=jnp.int32))
```

```python
import jax
import jax.numpy as jnp
from jax import lax
from jax.experimental import pallas as pl
from jax.experimental.pallas import tpu as pltpu
from jax.sharding import Mesh, PartitionSpec as P

SITES = 4
NU_SITE = 12
NT = 5
BS = 64
NOB = 32
LANES = 128
NSRC = 128
BUCKETS = SITES * NU_SITE
BLK = 1024
SUB = BLK // LANES
UNIT = NT * SUB
ALL_MU = ("yl", "c", "z", "yh")
FIT = ("x", "yl", "c")


def piece_kernel(mu_ref, slab_ref, *refs):
    coeff_refs, out_ref, scr = refs[:NT], refs[NT], refs[NT + 1]
    for t in range(NT):
        res = lax.dot_general(
            coeff_refs[t][...],
            slab_ref[t],
            (((0,), (0,)), ((), ())),
            preferred_element_type=jnp.float32,
        )
        for j in range(SUB):
            scr[pl.ds(t * SUB + j, NOB, stride=UNIT), :] = res[:, j * LANES : (j + 1) * LANES]
    out_ref[...] = scr[...].astype(jnp.bfloat16)


def make_pieces(three_center, mu_list, coeff):
    def coeff_map(t):
        return lambda q, mu: (mu[t], 0)

    return pl.pallas_call(
        piece_kernel,
        grid_spec=pltpu.PrefetchScalarGridSpec(
            num_scalar_prefetch=1,
            grid=(SITES,),
            in_specs=[pl.BlockSpec((NT, BS, BLK), lambda q, mu: (0, 0, q))]
            + [pl.BlockSpec((BS, NOB), coeff_map(t)) for t in range(NT)],
            out_specs=pl.BlockSpec((NOB * UNIT, LANES), lambda q, mu: (q, 0)),
            scratch_shapes=[pltpu.VMEM((NOB * UNIT, LANES), jnp.float32)],
        ),
        out_shape=jax.ShapeDtypeStruct((SITES * NOB * UNIT, LANES), jnp.bfloat16),
        compiler_params=pltpu.CompilerParams(vmem_limit_bytes=32 * 2**20),
        cost_estimate=pl.CostEstimate(
            flops=2 * NT * BS * NOB * 4096, bytes_accessed=4 * 2**20, transcendentals=0
        ),
        name="pieces",
    )(mu_list, three_center, *([coeff] * NT))


NACC = 4


def sum_kernel(key_ref, in_ref, out_ref, *accs):
    for acc in accs:
        acc[...] = jnp.zeros_like(acc)

    @pl.loop(0, NSRC * NT // 16)
    def _(i):
        for pair in range(8):
            two = in_ref[pl.ds(pl.multiple_of(i * (16 * SUB) + pair * 16, 16), 16), :].astype(jnp.float32)
            for half in range(2):
                acc = accs[(pair * 2 + half) % NACC]
                row = key_ref[i * 16 + pair * 2 + half] * SUB
                where = pl.ds(pl.multiple_of(row, SUB), SUB)
                acc[where, :] = acc[where, :] + two[half * SUB : (half + 1) * SUB]

    total = accs[0][...]
    for acc in accs[1:]:
        total = total + acc[...]
    total = total.astype(jnp.bfloat16)
    for x in range(4):
        out_ref[x] = total


def make_sums(keys, arrived):
    return pl.pallas_call(
        sum_kernel,
        in_specs=[
            pl.BlockSpec(memory_space=pltpu.SMEM),
            pl.BlockSpec(memory_space=pltpu.VMEM),
        ],
        out_specs=pl.BlockSpec(memory_space=pltpu.VMEM),
        out_shape=jax.ShapeDtypeStruct((4, BUCKETS * SUB, LANES), jnp.bfloat16),
        scratch_shapes=[pltpu.VMEM((BUCKETS * SUB, LANES), jnp.float32)] * NACC,
        compiler_params=pltpu.CompilerParams(vmem_limit_bytes=32 * 2**20),
        cost_estimate=pl.CostEstimate(
            flops=NSRC * NT * BLK, bytes_accessed=2 * 2**20, transcendentals=0
        ),
        name="sums",
    )(keys, arrived)


def fit_kernel(in_ref, weight_ref, out_ref):
    for k in range(NU_SITE):
        rows = [
            jnp.concatenate([in_ref[x, q, pl.ds(k * SUB, SUB), :] for q in range(4)], axis=0)
            for x in range(4)
        ]
        left = jnp.concatenate(rows, axis=1)
        res = lax.dot_general(
            left, weight_ref[k], (((1,), (1,)), ((), ())), preferred_element_type=jnp.float32
        )
        out_ref[k] = res.astype(jnp.bfloat16)


def make_fit(gathered, weights):
    return pl.pallas_call(
        fit_kernel,
        in_specs=[pl.BlockSpec(memory_space=pltpu.VMEM)] * 2,
        out_specs=pl.BlockSpec(memory_space=pltpu.VMEM),
        out_shape=jax.ShapeDtypeStruct((NU_SITE, 32, LANES), jnp.bfloat16),
        compiler_params=pltpu.CompilerParams(vmem_limit_bytes=32 * 2**20),
        name="fit",
    )(gathered, weights)


def local(three_center, pair_mu, pair_site, pair_pos, coeff, fitting):
    keys = pair_site[:, :, 0] * NU_SITE + pair_pos
    keys = jnp.pad(keys, ((0, 0), (0, LANES - NT)))
    all_keys = lax.all_gather(keys, ALL_MU, axis=0, tiled=True)
    all_keys = all_keys[:, :NT].reshape(-1)
    pieces = make_pieces(three_center, pair_mu[0], coeff)
    arrived = lax.all_to_all(pieces, ALL_MU, split_axis=0, concat_axis=0, tiled=True)
    site = lax.axis_index("yl") * 2 + lax.axis_index("c")
    weights = lax.dynamic_slice_in_dim(fitting, site * NU_SITE, NU_SITE, 0)
    same = jnp.eye(2, dtype=jnp.bfloat16)
    weights = weights.reshape(NU_SITE, 1, 64, 4, 1, 64) * same.reshape(1, 2, 1, 1, 2, 1)
    weights = weights.reshape(NU_SITE, LANES, 4 * LANES)
    sums = make_sums(all_keys, arrived)
    gathered = lax.all_to_all(
        sums.reshape(16, NU_SITE * SUB, LANES), FIT, split_axis=0, concat_axis=0, tiled=True
    )
    result = make_fit(gathered.reshape(4, 4, NU_SITE * SUB, LANES), weights)
    return result.reshape(1, NU_SITE, 1, 4096)


def solution(mesh):
    fine = Mesh(mesh.devices.reshape(8, 4, 2, 2, 4), ("z", "yh", "yl", "c", "x"))
    mu = ("z", "yh", "yl", "c")
    in_specs = (
        P(mu, None, "x"),
        P(mu, None),
        P(mu, None, None),
        P(mu, None),
        P(),
        P(None, "x", None),
    )
    out_specs = P(mu, None, None, "x")
    return jax.shard_map(local, mesh=fine, in_specs=in_specs, out_specs=out_specs, check_vma=False)
```

```python
import jax
import jax.numpy as jnp
from jax import lax
from jax.experimental import pallas as pl
from jax.experimental.pallas import tpu as pltpu
from jax.sharding import Mesh, PartitionSpec as P

SITES = 4
NU_SITE = 12
NT = 5
BS = 64
NOB = 32
LANES = 128
NSRC = 128
BUCKETS = SITES * NU_SITE
BLK = 1024
SUB = BLK // LANES
UNIT = (NT + 1) * SUB
ALL_MU = ("yl", "c", "z", "yh")
FIT = ("x", "yl", "c")
MIB = 2**20


def piece_kernel(mu_ref, site_ref, pos_ref, row_ref, slab_ref, *refs):
    coeff_refs, out_ref, scr = refs[:NT], refs[NT], refs[NT + 1]

    @pl.when(pl.program_id(0) == 0)
    def _():
        lane = lax.broadcasted_iota(jnp.int32, (SUB, LANES), 1)
        row = lax.broadcasted_iota(jnp.int32, (SUB, LANES), 0)
        tile = jnp.zeros((SUB, LANES), jnp.int32)
        for t in range(NT):
            tile = jnp.where(lane == t, site_ref[t] * NU_SITE + pos_ref[t], tile)
        tile = jnp.where(row == row_ref[0], tile, 0).astype(jnp.float32)
        for o in range(NOB):
            scr[o * UNIT + NT * SUB : (o + 1) * UNIT, :] = tile

    for t in range(NT):
        both = coeff_refs[t][...].astype(jnp.float32)
        mine = jnp.where(mu_ref[t] % 2 == 1, both[:, BS:], both[:, :BS]).astype(jnp.bfloat16)
        res = jnp.dot(mine, slab_ref[t], preferred_element_type=jnp.float32)
        for j in range(SUB):
            scr[pl.ds(t * SUB + j, NOB, stride=UNIT), :] = res[:, j * LANES : (j + 1) * LANES]
    out_ref[...] = scr[...].astype(jnp.bfloat16)


def make_pieces(three_center, pair_mu, pair_site, pair_pos, row, coeff):
    def coeff_map(t):
        return lambda q, mu, site, pos, row: (0, mu[t] // 2)

    return pl.pallas_call(
        piece_kernel,
        grid_spec=pltpu.PrefetchScalarGridSpec(
            num_scalar_prefetch=4,
            grid=(SITES,),
            in_specs=[pl.BlockSpec((NT, BS, BLK), lambda q, *_: (0, 0, q))]
            + [pl.BlockSpec((NOB, 2 * BS), coeff_map(t)) for t in range(NT)],
            out_specs=pl.BlockSpec((NOB * UNIT, LANES), lambda q, *_: (q, 0)),
            scratch_shapes=[pltpu.VMEM((NOB * UNIT, LANES), jnp.float32)],
        ),
        out_shape=jax.ShapeDtypeStruct((SITES * NOB * UNIT, LANES), jnp.bfloat16),
        compiler_params=pltpu.CompilerParams(vmem_limit_bytes=32 * MIB),
        cost_estimate=pl.CostEstimate(
            flops=2 * NT * BS * NOB * 4096, bytes_accessed=4 * MIB, transcendentals=0
        ),
        name="pieces",
    )(pair_mu, pair_site, pair_pos, row, three_center, *([coeff.T] * NT))


NACC = 4


def sum_kernel(in_ref, out_ref, keys_vmem, keys_smem, sem, *accs):
    for g in range(NSRC // SUB):
        tile = jnp.zeros((SUB, LANES), jnp.float32)
        for r in range(SUB):
            start = (g * SUB + r) * UNIT + NT * SUB
            tile = tile + in_ref[start - SUB : start + SUB, :].astype(jnp.float32)[SUB:]
        keys_vmem[g * SUB : (g + 1) * SUB, :] = tile.astype(jnp.int32)
    copy = pltpu.make_async_copy(keys_vmem, keys_smem, sem)
    copy.start()
    for acc in accs:
        acc[...] = jnp.zeros_like(acc)
    copy.wait()

    @pl.loop(0, NSRC // 4)
    def _(i):
        for s in range(4):
            source = i * 4 + s
            for pair in range((NT + 1) // 2):
                start = pl.multiple_of(source * UNIT + pair * 2 * SUB, 2 * SUB)
                two = in_ref[pl.ds(start, 2 * SUB), :].astype(jnp.float32)
                for half in range(2):
                    t = pair * 2 + half
                    if t < NT:
                        acc = accs[(s * NT + t) % NACC]
                        where = pl.ds(pl.multiple_of(keys_smem[source, t] * SUB, SUB), SUB)
                        acc[where, :] = acc[where, :] + two[half * SUB : (half + 1) * SUB]

    total = accs[0][...]
    for acc in accs[1:]:
        total = total + acc[...]
    total = total.astype(jnp.bfloat16)
    for x in range(4):
        out_ref[x] = total


def make_sums(arrived):
    return pl.pallas_call(
        sum_kernel,
        in_specs=[pl.BlockSpec(memory_space=pltpu.VMEM)],
        out_specs=pl.BlockSpec(memory_space=pltpu.VMEM),
        out_shape=jax.ShapeDtypeStruct((4, BUCKETS * SUB, LANES), jnp.bfloat16),
        scratch_shapes=[
            pltpu.VMEM((NSRC, LANES), jnp.int32),
            pltpu.SMEM((NSRC, LANES), jnp.int32),
            pltpu.SemaphoreType.DMA,
        ]
        + [pltpu.VMEM((BUCKETS * SUB, LANES), jnp.float32)] * NACC,
        compiler_params=pltpu.CompilerParams(vmem_limit_bytes=32 * MIB),
        cost_estimate=pl.CostEstimate(
            flops=NSRC * NT * BLK, bytes_accessed=2 * MIB, transcendentals=0
        ),
        name="sums",
    )(arrived)


HALF = LANES // 2
NHI = 32
KPAD = 16


def fit_kernel(site_ref, in_ref, weight_ref, out_ref, scr):
    for k in range(NU_SITE):
        rows = [
            jnp.concatenate([in_ref[x, q, pl.ds(k * SUB, SUB), :] for q in range(4)], axis=0)
            for x in range(4)
        ]
        low = jnp.concatenate([r[:, :HALF] for r in rows], axis=1)
        high = jnp.concatenate([r[:, HALF:] for r in rows], axis=1)
        res = lax.dot_general(
            jnp.concatenate([low, high], axis=0),
            weight_ref[k],
            (((1,), (1,)), ((), ())),
            preferred_element_type=jnp.float32,
        )
        scr[pl.ds(k, NHI, stride=KPAD), :] = jnp.concatenate([res[:NHI], res[NHI:]], axis=1)
    for n in range(NHI):
        out_ref[:, n * LANES : (n + 1) * LANES] = scr[n * KPAD : n * KPAD + NU_SITE, :].astype(
            jnp.bfloat16
        )


def make_fit(site, gathered, fitting):
    return pl.pallas_call(
        fit_kernel,
        grid_spec=pltpu.PrefetchScalarGridSpec(
            num_scalar_prefetch=1,
            grid=(1,),
            in_specs=[
                pl.BlockSpec((4, 4, NU_SITE * SUB, LANES), lambda i, site: (0, 0, 0, 0)),
                pl.BlockSpec((NU_SITE, 64, 256), lambda i, site: (site[0], 0, 0)),
            ],
            out_specs=pl.BlockSpec((NU_SITE, NHI * LANES), lambda i, site: (0, 0)),
            scratch_shapes=[pltpu.VMEM((NHI * KPAD, LANES), jnp.float32)],
        ),
        out_shape=jax.ShapeDtypeStruct((NU_SITE, NHI * LANES), jnp.bfloat16),
        compiler_params=pltpu.CompilerParams(vmem_limit_bytes=32 * MIB),
        name="fit",
    )(site, gathered, fitting)


def local(three_center, pair_mu, pair_site, pair_pos, coeff, fitting):
    row = (lax.axis_index("z") * 4 + lax.axis_index("yh")) % SUB
    pieces = make_pieces(
        three_center, pair_mu[0], pair_site[0, :, 0], pair_pos[0], row.reshape(1), coeff
    )
    arrived = lax.all_to_all(pieces, ALL_MU, split_axis=0, concat_axis=0, tiled=True)
    sums = make_sums(arrived)
    gathered = lax.all_to_all(
        sums.reshape(16, NU_SITE * SUB, LANES), FIT, split_axis=0, concat_axis=0, tiled=True
    )
    site = lax.axis_index("yl") * 2 + lax.axis_index("c")
    result = make_fit(site.reshape(1), gathered.reshape(4, 4, NU_SITE * SUB, LANES), fitting)
    return result.reshape(1, NU_SITE, 1, 4096)


def solution(mesh):
    fine = Mesh(mesh.devices.reshape(8, 4, 2, 2, 4), ("z", "yh", "yl", "c", "x"))
    mu = ("z", "yh", "yl", "c")
    in_specs = (
        P(mu, None, "x"),
        P(mu, None),
        P(mu, None, None),
        P(mu, None),
        P(),
        P(None, "x", None),
    )
    out_specs = P(mu, None, None, "x")
    return jax.shard_map(local, mesh=fine, in_specs=in_specs, out_specs=out_specs, check_vma=False)
```

```python
import jax
import jax.numpy as jnp
from jax import lax
from jax.experimental import pallas as pl
from jax.experimental.pallas import tpu as pltpu
from jax.sharding import Mesh, PartitionSpec as P

SITES = 4
NU_SITE = 12
NT = 5
BS = 64
NOB = 32
LANES = 128
NSRC = 64
CORES = 2
BUCKETS = SITES * NU_SITE
BLK = 1024
SUB = BLK // LANES
PAIR = 2 * SUB
UNIT = NT * PAIR + SUB
MAIN = ("yl", "z", "yh")
FIT = ("x", "yl", "c")
MIB = 2**20


def piece_kernel(mu_ref, site_ref, pos_ref, row_ref, slab_ref, *refs):
    coeff_refs, out_ref, scr = refs[:NT], refs[NT], refs[NT + 1]
    step = pl.program_id(0)

    @pl.when(step == 0)
    def _():
        lane = lax.broadcasted_iota(jnp.int32, (SUB, LANES), 1)
        row = lax.broadcasted_iota(jnp.int32, (SUB, LANES), 0)
        tile = jnp.zeros((SUB, LANES), jnp.int32)
        for t in range(NT):
            tile = jnp.where(lane == t, site_ref[t] * NU_SITE + pos_ref[t], tile)
        tile = jnp.where(row == row_ref[0], tile, 0).astype(jnp.float32)
        for o in range(NOB):
            scr[o * UNIT + NT * PAIR : (o + 1) * UNIT, :] = tile

    def fill(half):
        for t in range(NT):
            both = coeff_refs[t][...].astype(jnp.float32)
            mine = jnp.where(mu_ref[t] % 2 == 1, both[:, BS:], both[:, :BS]).astype(jnp.bfloat16)
            res = jnp.dot(mine, slab_ref[t], preferred_element_type=jnp.float32)
            for j in range(SUB):
                scr[pl.ds(t * PAIR + half * SUB + j, NOB, stride=UNIT), :] = res[
                    :, j * LANES : (j + 1) * LANES
                ]

    @pl.when(step % 2 == 0)
    def _():
        fill(0)

    @pl.when(step % 2 == 1)
    def _():
        fill(1)
        out_ref[...] = scr[...].astype(jnp.bfloat16)


def make_pieces(three_center, pair_mu, pair_site, pair_pos, row, coeff):
    def coeff_map(t):
        return lambda q, mu, site, pos, row: (0, mu[t] // 2)

    return pl.pallas_call(
        piece_kernel,
        grid_spec=pltpu.PrefetchScalarGridSpec(
            num_scalar_prefetch=4,
            grid=(SITES,),
            in_specs=[pl.BlockSpec((NT, BS, BLK), lambda q, *_: (0, 0, q))]
            + [pl.BlockSpec((NOB, 2 * BS), coeff_map(t)) for t in range(NT)],
            out_specs=pl.BlockSpec((NOB * UNIT, LANES), lambda q, *_: (q // 2, 0)),
            scratch_shapes=[pltpu.VMEM((NOB * UNIT, LANES), jnp.float32)],
        ),
        out_shape=jax.ShapeDtypeStruct((2 * NOB * UNIT, LANES), jnp.bfloat16),
        compiler_params=pltpu.CompilerParams(vmem_limit_bytes=58 * MIB),
        cost_estimate=pl.CostEstimate(
            flops=2 * NT * BS * NOB * 4096, bytes_accessed=4 * MIB, transcendentals=0
        ),
        name="pieces",
    )(pair_mu, pair_site, pair_pos, row, three_center, *([coeff.T] * NT))


COPIES = 2
DUO = 2 * UNIT


def sum_kernel(core_ref, in_ref, keep_ref, send_ref, keys_vmem, keys_smem, sem, *accs):
    tiles = UNIT // SUB
    for g in range(NSRC // SUB):
        tile = jnp.zeros((SUB, LANES), jnp.float32)
        for r in range(0, SUB, 2):
            start = (g * SUB + r) * UNIT
            first = in_ref[start + NT * PAIR : start + NT * PAIR + PAIR, :].astype(jnp.float32)
            second = in_ref[start + DUO - PAIR : start + DUO, :].astype(jnp.float32)
            tile = tile + first[:SUB] + second[SUB:]
        keys_vmem[g * SUB : (g + 1) * SUB, :] = tile.astype(jnp.int32)
    copy = pltpu.make_async_copy(keys_vmem, keys_smem, sem)
    copy.start()
    for acc in accs:
        acc[...] = jnp.zeros_like(acc)
    copy.wait()

    @pl.loop(0, NSRC // 4)
    def _(i):
        for d in range(2):
            for pair in range(tiles):
                start = pl.multiple_of((i * 2 + d) * DUO + pair * PAIR, PAIR)
                two = in_ref[pl.ds(start, PAIR), :].astype(jnp.float32)
                for part in range(2):
                    which, place = divmod(pair * 2 + part, tiles)
                    t, half = divmod(place, 2)
                    if t < NT:
                        acc = accs[half * COPIES + (which + t) % COPIES]
                        row = keys_smem[i * 4 + d * 2 + which, t] * SUB
                        where = pl.ds(pl.multiple_of(row, SUB), SUB)
                        acc[where, :] = acc[where, :] + two[part * SUB : (part + 1) * SUB]

    left = accs[0][...] + accs[1][...]
    right = accs[2][...] + accs[3][...]
    first_core = core_ref[0] == 0
    keep_ref[...] = jnp.where(first_core, left, right)
    send_ref[...] = jnp.where(first_core, right, left)


def make_sums(core, arrived):
    half = jax.ShapeDtypeStruct((BUCKETS * SUB, LANES), jnp.float32)
    return pl.pallas_call(
        sum_kernel,
        in_specs=[
            pl.BlockSpec(memory_space=pltpu.SMEM),
            pl.BlockSpec(memory_space=pltpu.VMEM),
        ],
        out_specs=[pl.BlockSpec(memory_space=pltpu.VMEM)] * 2,
        out_shape=[half, half],
        scratch_shapes=[
            pltpu.VMEM((NSRC, LANES), jnp.int32),
            pltpu.SMEM((NSRC, LANES), jnp.int32),
            pltpu.SemaphoreType.DMA,
        ]
        + [pltpu.VMEM((BUCKETS * SUB, LANES), jnp.float32)] * (2 * COPIES),
        compiler_params=pltpu.CompilerParams(vmem_limit_bytes=32 * MIB),
        cost_estimate=pl.CostEstimate(
            flops=NSRC * NT * 2 * BLK, bytes_accessed=2 * MIB, transcendentals=0
        ),
        name="sums",
    )(core, arrived)


def join_kernel(keep_ref, got_ref, out_ref):
    total = (keep_ref[...] + got_ref[...]).astype(jnp.bfloat16)
    for x in range(4):
        out_ref[x] = total


def make_join(keep, got):
    return pl.pallas_call(
        join_kernel,
        in_specs=[pl.BlockSpec(memory_space=pltpu.VMEM)] * 2,
        out_specs=pl.BlockSpec(memory_space=pltpu.VMEM),
        out_shape=jax.ShapeDtypeStruct((4, BUCKETS * SUB, LANES), jnp.bfloat16),
        compiler_params=pltpu.CompilerParams(vmem_limit_bytes=32 * MIB),
        name="join",
    )(keep, got)


HALF = LANES // 2
NHI = 32
KPAD = 16


def fit_kernel(site_ref, in_ref, weight_ref, out_ref, scr):
    for k in range(NU_SITE):
        rows = [
            jnp.concatenate([in_ref[x, q, pl.ds(k * SUB, SUB), :] for q in range(4)], axis=0)
            for x in range(4)
        ]
        low = jnp.concatenate([r[:, :HALF] for r in rows], axis=1)
        high = jnp.concatenate([r[:, HALF:] for r in rows], axis=1)
        res = lax.dot_general(
            jnp.concatenate([low, high], axis=0),
            weight_ref[k],
            (((1,), (1,)), ((), ())),
            preferred_element_type=jnp.float32,
        )
        scr[pl.ds(k, NHI, stride=KPAD), :] = jnp.concatenate([res[:NHI], res[NHI:]], axis=1)
    for n in range(NHI):
        out_ref[:, n * LANES : (n + 1) * LANES] = scr[n * KPAD : n * KPAD + NU_SITE, :].astype(
            jnp.bfloat16
        )


def make_fit(site, gathered, fitting):
    return pl.pallas_call(
        fit_kernel,
        grid_spec=pltpu.PrefetchScalarGridSpec(
            num_scalar_prefetch=1,
            grid=(1,),
            in_specs=[
                pl.BlockSpec((4, 4, NU_SITE * SUB, LANES), lambda i, site: (0, 0, 0, 0)),
                pl.BlockSpec((NU_SITE, 64, 256), lambda i, site: (site[0], 0, 0)),
            ],
            out_specs=pl.BlockSpec((NU_SITE, NHI * LANES), lambda i, site: (0, 0)),
            scratch_shapes=[pltpu.VMEM((NHI * KPAD, LANES), jnp.float32)],
        ),
        out_shape=jax.ShapeDtypeStruct((NU_SITE, NHI * LANES), jnp.bfloat16),
        compiler_params=pltpu.CompilerParams(vmem_limit_bytes=32 * MIB),
        name="fit",
    )(site, gathered, fitting)


def local(three_center, pair_mu, pair_site, pair_pos, coeff, fitting):
    row = (lax.axis_index("z") * 4 + lax.axis_index("yh")) % SUB
    pieces = make_pieces(
        three_center, pair_mu[0], pair_site[0, :, 0], pair_pos[0], row.reshape(1), coeff
    )
    arrived = lax.all_to_all(pieces, MAIN, split_axis=0, concat_axis=0, tiled=True)
    keep, send = make_sums(lax.axis_index("c").reshape(1), arrived)
    got = lax.ppermute(send, "c", [(0, 1), (1, 0)])
    sums = make_join(keep, got)
    gathered = lax.all_to_all(
        sums.reshape(16, NU_SITE * SUB, LANES), FIT, split_axis=0, concat_axis=0, tiled=True
    )
    site = lax.axis_index("yl") * 2 + lax.axis_index("c")
    result = make_fit(site.reshape(1), gathered.reshape(4, 4, NU_SITE * SUB, LANES), fitting)
    return result.reshape(1, NU_SITE, 1, 4096)


def solution(mesh):
    fine = Mesh(mesh.devices.reshape(8, 4, 2, 2, 4), ("z", "yh", "yl", "c", "x"))
    mu = ("z", "yh", "yl", "c")
    in_specs = (
        P(mu, None, "x"),
        P(mu, None),
        P(mu, None, None),
        P(mu, None),
        P(),
        P(None, "x", None),
    )
    out_specs = P(mu, None, None, "x")
    return jax.shard_map(local, mesh=fine, in_specs=in_specs, out_specs=out_specs, check_vma=False)
```

```python
import jax
import jax.numpy as jnp
from jax import lax
from jax.experimental import pallas as pl
from jax.experimental.pallas import tpu as pltpu
from jax.sharding import Mesh, PartitionSpec as P

SITES = 4
NU_SITE = 12
NT = 5
BS = 64
NOB = 32
LANES = 128
NSRC = 128
BUCKETS = SITES * NU_SITE
BLK = 1024
SUB = BLK // LANES
UNIT = NT * SUB
ALL_MU = ("yl", "c", "zh", "zl", "yh")
FIT = ("x", "yl", "c")
MIB = 2**20


def piece_kernel(mu_hbm, slab_hbm, coeff_hbm, out_hbm, mu, slab, coeff, scr, done, small, ins, outs):
    def slab_copy(q):
        return pltpu.make_async_copy(
            slab_hbm.at[:, :, pl.ds(q * BLK, BLK)], slab.at[q], ins.at[q]
        )

    def out_copy(q):
        rows = pl.ds(q * NOB * UNIT, NOB * UNIT)
        return pltpu.make_async_copy(done.at[q], out_hbm.at[rows, :], outs.at[q])

    mu_copy = pltpu.make_async_copy(mu_hbm, mu, small.at[0])
    coeff_copy = pltpu.make_async_copy(coeff_hbm, coeff, small.at[1])
    mu_copy.start()
    coeff_copy.start()
    for q in range(SITES):
        slab_copy(q).start()
    mu_copy.wait()
    coeff_copy.wait()
    mine = []
    for t in range(NT):
        block = mu[0, t]
        both = coeff[:, pl.ds(pl.multiple_of(block // 2 * LANES, LANES), LANES)].astype(jnp.float32)
        mine.append(
            jnp.where(block % 2 == 1, both[:, BS:], both[:, :BS]).astype(jnp.bfloat16)
        )
    for q in range(SITES):
        slab_copy(q).wait()
        for t in range(NT):
            res = jnp.dot(mine[t], slab[q, t], preferred_element_type=jnp.float32)
            for j in range(SUB):
                scr[pl.ds(t * SUB + j, NOB, stride=UNIT), :] = res[
                    :, j * LANES : (j + 1) * LANES
                ]
        done[q] = scr[...].astype(jnp.bfloat16)
        out_copy(q).start()
    for q in range(SITES):
        out_copy(q).wait()


def make_pieces(three_center, pair_mu, coeff):
    return pl.pallas_call(
        piece_kernel,
        in_specs=[pl.BlockSpec(memory_space=pl.ANY)] * 3,
        out_specs=pl.BlockSpec(memory_space=pl.ANY),
        out_shape=jax.ShapeDtypeStruct((SITES * NOB * UNIT, LANES), jnp.bfloat16),
        scratch_shapes=[
            pltpu.SMEM((1, NT), jnp.int32),
            pltpu.VMEM((SITES, NT, BS, BLK), jnp.bfloat16),
            pltpu.VMEM((NOB, 3072), jnp.bfloat16),
            pltpu.VMEM((NOB * UNIT, LANES), jnp.float32),
            pltpu.VMEM((SITES, NOB * UNIT, LANES), jnp.bfloat16),
            pltpu.SemaphoreType.DMA((2,)),
            pltpu.SemaphoreType.DMA((SITES,)),
            pltpu.SemaphoreType.DMA((SITES,)),
        ],
        compiler_params=pltpu.CompilerParams(vmem_limit_bytes=58 * MIB),
        cost_estimate=pl.CostEstimate(
            flops=2 * NT * BS * NOB * 4096, bytes_accessed=4 * MIB, transcendentals=0
        ),
        name="pieces",
    )(pair_mu, three_center, coeff.T)


NACC = 4


def sum_kernel(key_ref, in_ref, out_ref, *accs):
    for acc in accs:
        acc[...] = jnp.zeros_like(acc)

    @pl.loop(0, NSRC // 4)
    def _(i):
        for pair in range(2 * NT):
            start = pl.multiple_of(i * 4 * UNIT + pair * 2 * SUB, 2 * SUB)
            two = in_ref[pl.ds(start, 2 * SUB), :].astype(jnp.float32)
            for half in range(2):
                which, t = divmod(pair * 2 + half, NT)
                acc = accs[(pair * 2 + half) % NACC]
                where = pl.ds(pl.multiple_of(key_ref[i * 4 + which, t] * SUB, SUB), SUB)
                acc[where, :] = acc[where, :] + two[half * SUB : (half + 1) * SUB]

    total = accs[0][...]
    for acc in accs[1:]:
        total = total + acc[...]
    total = total.astype(jnp.bfloat16)
    for x in range(4):
        out_ref[x] = total


def make_sums(keys, arrived):
    return pl.pallas_call(
        sum_kernel,
        in_specs=[
            pl.BlockSpec(memory_space=pltpu.SMEM),
            pl.BlockSpec(memory_space=pltpu.VMEM),
        ],
        out_specs=pl.BlockSpec(memory_space=pltpu.VMEM),
        out_shape=jax.ShapeDtypeStruct((4, BUCKETS * SUB, LANES), jnp.bfloat16),
        scratch_shapes=[pltpu.VMEM((BUCKETS * SUB, LANES), jnp.float32)] * NACC,
        compiler_params=pltpu.CompilerParams(vmem_limit_bytes=32 * MIB),
        cost_estimate=pl.CostEstimate(
            flops=NSRC * NT * BLK, bytes_accessed=2 * MIB, transcendentals=0
        ),
        name="sums",
    )(keys, arrived)


HALF = LANES // 2
NHI = 32
KPAD = 16


def fit_kernel(site_ref, in_ref, weight_ref, out_ref, scr):
    for k in range(NU_SITE):
        rows = [
            jnp.concatenate([in_ref[x, q, pl.ds(k * SUB, SUB), :] for q in range(4)], axis=0)
            for x in range(4)
        ]
        low = jnp.concatenate([r[:, :HALF] for r in rows], axis=1)
        high = jnp.concatenate([r[:, HALF:] for r in rows], axis=1)
        res = lax.dot_general(
            jnp.concatenate([low, high], axis=0),
            weight_ref[k],
            (((1,), (1,)), ((), ())),
            preferred_element_type=jnp.float32,
        )
        scr[pl.ds(k, NHI, stride=KPAD), :] = jnp.concatenate([res[:NHI], res[NHI:]], axis=1)
    for n in range(NHI):
        out_ref[:, n * LANES : (n + 1) * LANES] = scr[n * KPAD : n * KPAD + NU_SITE, :].astype(
            jnp.bfloat16
        )


def make_fit(site, gathered, fitting):
    return pl.pallas_call(
        fit_kernel,
        grid_spec=pltpu.PrefetchScalarGridSpec(
            num_scalar_prefetch=1,
            grid=(1,),
            in_specs=[
                pl.BlockSpec((4, 4, NU_SITE * SUB, LANES), lambda i, site: (0, 0, 0, 0)),
                pl.BlockSpec((NU_SITE, 64, 256), lambda i, site: (site[0], 0, 0)),
            ],
            out_specs=pl.BlockSpec((NU_SITE, NHI * LANES), lambda i, site: (0, 0)),
            scratch_shapes=[pltpu.VMEM((NHI * KPAD, LANES), jnp.float32)],
        ),
        out_shape=jax.ShapeDtypeStruct((NU_SITE, NHI * LANES), jnp.bfloat16),
        compiler_params=pltpu.CompilerParams(vmem_limit_bytes=32 * MIB),
        name="fit",
    )(site, gathered, fitting)


def local(three_center, pair_mu, pair_site, pair_pos, coeff, fitting):
    pieces = make_pieces(three_center, pair_mu, coeff)
    keys = jnp.pad(pair_site[:, :, 0] * NU_SITE + pair_pos, ((0, 0), (0, LANES - NT)))
    for axis in reversed(ALL_MU):
        keys = lax.all_gather(keys, axis, axis=0, tiled=True)
    arrived = lax.all_to_all(pieces, ALL_MU, split_axis=0, concat_axis=0, tiled=True)
    sums = make_sums(keys, arrived)
    gathered = lax.all_to_all(
        sums.reshape(16, NU_SITE * SUB, LANES), FIT, split_axis=0, concat_axis=0, tiled=True
    )
    site = lax.axis_index("yl") * 2 + lax.axis_index("c")
    result = make_fit(site.reshape(1), gathered.reshape(4, 4, NU_SITE * SUB, LANES), fitting)
    return result.reshape(1, NU_SITE, 1, 4096)


def solution(mesh):
    fine = Mesh(mesh.devices.reshape(4, 2, 4, 2, 2, 4), ("zh", "zl", "yh", "yl", "c", "x"))
    mu = ("zh", "zl", "yh", "yl", "c")
    in_specs = (
        P(mu, None, "x"),
        P(mu, None),
        P(mu, None, None),
        P(mu, None),
        P(),
        P(None, "x", None),
    )
    out_specs = P(mu, None, None, "x")
    return jax.shard_map(local, mesh=fine, in_specs=in_specs, out_specs=out_specs, check_vma=False)
```

```python
import jax
import jax.numpy as jnp
from jax import lax
from jax.experimental import pallas as pl
from jax.experimental.pallas import tpu as pltpu
from jax.sharding import Mesh, PartitionSpec as P

SITES = 4
NU_SITE = 12
NT = 5
BS = 64
NOB = 32
LANES = 128
NSRC = 128
BUCKETS = SITES * NU_SITE
BLK = 1024
SUB = BLK // LANES
DATA = NT * SUB
UNIT = DATA + 2
ALL_MU = ("yl", "c", "z", "yh")
FIT = ("x", "yl", "c")
MIB = 2**20


def source_index():
    quarter = lax.axis_index("yl") * 2 + lax.axis_index("c")
    return (quarter * 8 + lax.axis_index("z")) * 4 + lax.axis_index("yh")


def piece_kernel(
    mu_hbm, site_hbm, pos_hbm, slab_hbm, coeff_hbm, out_hbm,
    mu, site, pos, slab, coeff, scr, done, small, ins, outs,
):
    def slab_copy(q):
        return pltpu.make_async_copy(
            slab_hbm.at[:, :, pl.ds(q * BLK, BLK)], slab.at[q], ins.at[q]
        )

    def out_copy(q):
        rows = pl.ds(q * NOB * UNIT, NOB * UNIT)
        return pltpu.make_async_copy(done.at[q], out_hbm.at[rows, :], outs.at[q])

    smalls = [
        pltpu.make_async_copy(src, dst, small.at[i])
        for i, (src, dst) in enumerate(
            [(mu_hbm, mu), (coeff_hbm, coeff), (site_hbm, site), (pos_hbm, pos)]
        )
    ]
    for copy in smalls:
        copy.start()
    for q in range(SITES):
        slab_copy(q).start()
    me = source_index()
    shift = me % 4 * 2
    first_lane = me // 8 * 8
    for copy in smalls:
        copy.wait()
    lane = lax.broadcasted_iota(jnp.int32, (NOB, LANES), 1)
    keys = jnp.zeros((NOB, LANES), jnp.int32)
    for t in range(NT):
        keys = jnp.where(lane == first_lane + t, site[0, t] * NU_SITE + pos[0, t], keys)
    for r in range(2):
        scr[pl.ds(DATA + r, NOB, stride=UNIT), :] = keys.astype(jnp.float32)
    mine = []
    for t in range(NT):
        block = mu[0, t]
        both = coeff[:, pl.ds(pl.multiple_of(block // 2 * LANES, LANES), LANES)].astype(jnp.float32)
        mine.append(
            jnp.where(block % 2 == 1, both[:, BS:], both[:, :BS]).astype(jnp.bfloat16)
        )
    for q in range(SITES):
        slab_copy(q).wait()
        for t in range(NT):
            res = jnp.dot(mine[t], slab[q, t], preferred_element_type=jnp.float32)
            for j in range(SUB):
                place = t * SUB + j - shift
                place = jnp.where(place < 0, place + DATA, place)
                scr[pl.ds(place, NOB, stride=UNIT), :] = res[
                    :, j * LANES : (j + 1) * LANES
                ]
        done[q] = scr[...].astype(jnp.bfloat16)
        out_copy(q).start()
    for q in range(SITES):
        out_copy(q).wait()


def make_pieces(three_center, pair_mu, pair_site, pair_pos, coeff):
    return pl.pallas_call(
        piece_kernel,
        in_specs=[pl.BlockSpec(memory_space=pl.ANY)] * 5,
        out_specs=pl.BlockSpec(memory_space=pl.ANY),
        out_shape=jax.ShapeDtypeStruct((SITES * NOB * UNIT, LANES), jnp.bfloat16),
        scratch_shapes=[
            pltpu.SMEM((1, NT), jnp.int32),
            pltpu.SMEM((1, NT), jnp.int32),
            pltpu.SMEM((1, NT), jnp.int32),
            pltpu.VMEM((SITES, NT, BS, BLK), jnp.bfloat16),
            pltpu.VMEM((NOB, 3072), jnp.bfloat16),
            pltpu.VMEM((NOB * UNIT, LANES), jnp.float32),
            pltpu.VMEM((SITES, NOB * UNIT, LANES), jnp.bfloat16),
            pltpu.SemaphoreType.DMA((4,)),
            pltpu.SemaphoreType.DMA((SITES,)),
            pltpu.SemaphoreType.DMA((SITES,)),
        ],
        compiler_params=pltpu.CompilerParams(vmem_limit_bytes=58 * MIB),
        cost_estimate=pl.CostEstimate(
            flops=2 * NT * BS * NOB * 4096, bytes_accessed=4 * MIB, transcendentals=0
        ),
        name="pieces",
    )(pair_mu, pair_site[:, :, 0], pair_pos, three_center, coeff.T)


NACC = 4


FOUR = 4 * UNIT // SUB


def sum_kernel(in_ref, out_ref, key_vmem, key_ref, sem, *accs):
    sub = lax.broadcasted_iota(jnp.int32, (SUB, LANES), 0)

    def tiles_of(two_blocks, wanted):
        found = {}
        for pair in sorted({tile // 2 for tile in wanted}):
            start = pl.multiple_of((two_blocks * FOUR + pair) * 2 * SUB, 2 * SUB)
            two = in_ref[pl.ds(start, 2 * SUB), :].astype(jnp.float32)
            found[pair * 2], found[pair * 2 + 1] = two[:SUB], two[SUB:]
        return found

    keys = jnp.zeros((SUB, LANES), jnp.float32)
    for u in range(NSRC // 8):
        found = tiles_of(u, [b * FOUR + 5 * m + 5 for b in range(2) for m in range(4)])
        for b in range(2):
            for m in range(4):
                keys = keys + jnp.where(sub == 2 * m + b, found[b * FOUR + 5 * m + 5], 0.0)
    key_vmem[...] = keys.astype(jnp.int32)
    copy = pltpu.make_async_copy(key_vmem, key_ref, sem)
    copy.start()
    for acc in accs:
        acc[...] = jnp.zeros_like(acc)
    copy.wait()

    @pl.loop(0, NSRC // 8)
    def _(u):
        found = tiles_of(u, range(2 * FOUR))
        for b in range(2):
            for m in range(4):
                for t in range(NT):
                    tile = found[b * FOUR + 5 * m + t]
                    if t == 0 and m > 0:
                        tile = jnp.where(sub >= 2 * m, tile, found[b * FOUR + 5 * m + 5])
                    acc = accs[(m + t) % NACC]
                    row = key_ref[2 * m + b, u * 8 + t] * SUB
                    where = pl.ds(pl.multiple_of(row, SUB), SUB)
                    acc[where, :] = acc[where, :] + tile

    total = accs[0][...]
    for acc in accs[1:]:
        total = total + acc[...]
    total = total.astype(jnp.bfloat16)
    for x in range(4):
        out_ref[x] = total


def make_sums(arrived):
    return pl.pallas_call(
        sum_kernel,
        in_specs=[
            pl.BlockSpec(memory_space=pltpu.VMEM),
        ],
        out_specs=pl.BlockSpec(memory_space=pltpu.VMEM),
        out_shape=jax.ShapeDtypeStruct((4, BUCKETS * SUB, LANES), jnp.bfloat16),
        scratch_shapes=[
            pltpu.VMEM((SUB, LANES), jnp.int32),
            pltpu.SMEM((SUB, LANES), jnp.int32),
            pltpu.SemaphoreType.DMA,
        ]
        + [pltpu.VMEM((BUCKETS * SUB, LANES), jnp.float32)] * NACC,
        compiler_params=pltpu.CompilerParams(vmem_limit_bytes=32 * MIB),
        cost_estimate=pl.CostEstimate(
            flops=NSRC * NT * BLK, bytes_accessed=2 * MIB, transcendentals=0
        ),
        name="sums",
    )(arrived)


HALF = LANES // 2
NHI = 32
KPAD = 16


def fit_kernel(site_ref, in_ref, weight_ref, out_ref, scr):
    for k in range(NU_SITE):
        rows = [
            jnp.concatenate([in_ref[x, q, pl.ds(k * SUB, SUB), :] for q in range(4)], axis=0)
            for x in range(4)
        ]
        low = jnp.concatenate([r[:, :HALF] for r in rows], axis=1)
        high = jnp.concatenate([r[:, HALF:] for r in rows], axis=1)
        res = lax.dot_general(
            jnp.concatenate([low, high], axis=0),
            weight_ref[k],
            (((1,), (1,)), ((), ())),
            preferred_element_type=jnp.float32,
        )
        scr[pl.ds(k, NHI, stride=KPAD), :] = jnp.concatenate([res[:NHI], res[NHI:]], axis=1)
    for n in range(NHI):
        out_ref[:, n * LANES : (n + 1) * LANES] = scr[n * KPAD : n * KPAD + NU_SITE, :].astype(
            jnp.bfloat16
        )


def make_fit(site, gathered, fitting):
    return pl.pallas_call(
        fit_kernel,
        grid_spec=pltpu.PrefetchScalarGridSpec(
            num_scalar_prefetch=1,
            grid=(1,),
            in_specs=[
                pl.BlockSpec((4, 4, NU_SITE * SUB, LANES), lambda i, site: (0, 0, 0, 0)),
                pl.BlockSpec((NU_SITE, 64, 256), lambda i, site: (site[0], 0, 0)),
            ],
            out_specs=pl.BlockSpec((NU_SITE, NHI * LANES), lambda i, site: (0, 0)),
            scratch_shapes=[pltpu.VMEM((NHI * KPAD, LANES), jnp.float32)],
        ),
        out_shape=jax.ShapeDtypeStruct((NU_SITE, NHI * LANES), jnp.bfloat16),
        compiler_params=pltpu.CompilerParams(vmem_limit_bytes=32 * MIB),
        name="fit",
    )(site, gathered, fitting)


def local(three_center, pair_mu, pair_site, pair_pos, coeff, fitting):
    pieces = make_pieces(three_center, pair_mu, pair_site, pair_pos, coeff)
    arrived = lax.all_to_all(
        pieces.reshape(NSRC, UNIT // 2, 2, LANES), ALL_MU, split_axis=0, concat_axis=0, tiled=True
    )
    sums = make_sums(arrived.reshape(NSRC * UNIT, LANES))
    gathered = lax.all_to_all(
        sums.reshape(16, NU_SITE * SUB, LANES), FIT, split_axis=0, concat_axis=0, tiled=True
    )
    site = lax.axis_index("yl") * 2 + lax.axis_index("c")
    result = make_fit(site.reshape(1), gathered.reshape(4, 4, NU_SITE * SUB, LANES), fitting)
    return result.reshape(1, NU_SITE, 1, 4096)


def solution(mesh):
    fine = Mesh(mesh.devices.reshape(8, 4, 2, 2, 4), ("z", "yh", "yl", "c", "x"))
    mu = ("z", "yh", "yl", "c")
    in_specs = (
        P(mu, None, "x"),
        P(mu, None),
        P(mu, None, None),
        P(mu, None),
        P(),
        P(None, "x", None),
    )
    out_specs = P(mu, None, None, "x")
    return jax.shard_map(local, mesh=fine, in_specs=in_specs, out_specs=out_specs, check_vma=False)
```

```python
import jax
import jax.numpy as jnp
from jax import lax
from jax.experimental import pallas as pl
from jax.experimental.pallas import tpu as pltpu
from jax.sharding import Mesh, PartitionSpec as P

SITES = 4
NU_SITE = 12
NT = 5
BS = 64
NOB = 32
LANES = 128
NSRC = 64
BUCKETS = SITES * NU_SITE
BLK = 1024
SUB = BLK // LANES
PAIR = 2 * SUB
DATA = NT * PAIR
UNIT = DATA + 2
MAIN = ("yl", "z", "yh")
FIT = ("x", "yl")
PART = NOB // 2 * UNIT
MIB = 2**20


def source_index():
    return (lax.axis_index("yl") * 8 + lax.axis_index("z")) * 4 + lax.axis_index("yh")


def piece_kernel(
    mu_hbm, site_hbm, pos_hbm, slab_hbm, coeff_hbm, out_hbm,
    mu, site, pos, slab, coeff, scr, done, small, ins, outs,
):
    def slab_copy(q):
        return pltpu.make_async_copy(
            slab_hbm.at[:, :, pl.ds(q * BLK, BLK)], slab.at[q], ins.at[q]
        )

    def out_copy(part):
        rows = pl.ds(part * PART, PART)
        return pltpu.make_async_copy(done.at[rows, :], out_hbm.at[rows, :], outs.at[part])

    smalls = [
        pltpu.make_async_copy(src, dst, small.at[i])
        for i, (src, dst) in enumerate(
            [(mu_hbm, mu), (coeff_hbm, coeff), (site_hbm, site), (pos_hbm, pos)]
        )
    ]
    for copy in smalls:
        copy.start()
    for q in range(SITES):
        slab_copy(q).start()
    me = source_index()
    shift = me % 4 * 2
    first_lane = me // 8 * 8
    for copy in smalls:
        copy.wait()
    lane = lax.broadcasted_iota(jnp.int32, (NOB, LANES), 1)
    keys = jnp.zeros((NOB, LANES), jnp.int32)
    for t in range(NT):
        keys = jnp.where(lane == first_lane + t, site[0, t] * NU_SITE + pos[0, t], keys)
    for r in range(2):
        scr[pl.ds(DATA + r, NOB, stride=UNIT), :] = keys.astype(jnp.float32)
    mine = []
    for t in range(NT):
        block = mu[0, t]
        both = coeff[:, pl.ds(pl.multiple_of(block // 2 * LANES, LANES), LANES)].astype(jnp.float32)
        mine.append(
            jnp.where(block % 2 == 1, both[:, BS:], both[:, :BS]).astype(jnp.bfloat16)
        )
    for q in range(SITES):
        column, half = divmod(q, 2)
        slab_copy(q).wait()
        for t in range(NT):
            res = jnp.dot(mine[t], slab[q, t], preferred_element_type=jnp.float32)
            for j in range(SUB):
                place = t * PAIR + half * SUB + j - shift
                place = jnp.where(place < 0, place + DATA, place)
                scr[pl.ds(place, NOB, stride=UNIT), :] = res[
                    :, j * LANES : (j + 1) * LANES
                ]
        if half == 1:
            for o in range(2):
                start = (column * 2 + o) * PART
                done[start : start + PART, :] = scr[o * PART : (o + 1) * PART, :].astype(
                    jnp.bfloat16
                )
                out_copy(column * 2 + o).start()
    for part in range(4):
        out_copy(part).wait()


def make_pieces(three_center, pair_mu, pair_site, pair_pos, coeff):
    return pl.pallas_call(
        piece_kernel,
        in_specs=[pl.BlockSpec(memory_space=pl.ANY)] * 5,
        out_specs=pl.BlockSpec(memory_space=pl.ANY),
        out_shape=jax.ShapeDtypeStruct((4 * PART, LANES), jnp.bfloat16),
        scratch_shapes=[
            pltpu.SMEM((1, NT), jnp.int32),
            pltpu.SMEM((1, NT), jnp.int32),
            pltpu.SMEM((1, NT), jnp.int32),
            pltpu.VMEM((SITES, NT, BS, BLK), jnp.bfloat16),
            pltpu.VMEM((NOB, 3072), jnp.bfloat16),
            pltpu.VMEM((NOB * UNIT, LANES), jnp.float32),
            pltpu.VMEM((4 * PART, LANES), jnp.bfloat16),
            pltpu.SemaphoreType.DMA((4,)),
            pltpu.SemaphoreType.DMA((SITES,)),
            pltpu.SemaphoreType.DMA((SITES,)),
        ],
        compiler_params=pltpu.CompilerParams(vmem_limit_bytes=58 * MIB),
        cost_estimate=pl.CostEstimate(
            flops=2 * NT * BS * NOB * 4096, bytes_accessed=4 * MIB, transcendentals=0
        ),
        name="pieces",
    )(pair_mu, pair_site[:, :, 0], pair_pos, three_center, coeff.T)


COPIES = 2
STEP = 2 * NT
FOUR = 4 * UNIT // SUB
SITE_ROWS = NU_SITE * SUB


def sum_kernel(in_ref, keep_ref, send_ref, key_vmem, key_ref, sem, *accs):
    sub = lax.broadcasted_iota(jnp.int32, (SUB, LANES), 0)

    def tiles_of(two_blocks, wanted):
        found = {}
        for pair in sorted({tile // 2 for tile in wanted}):
            start = pl.multiple_of((two_blocks * FOUR + pair) * 2 * SUB, 2 * SUB)
            two = in_ref[pl.ds(start, 2 * SUB), :].astype(jnp.float32)
            found[pair * 2], found[pair * 2 + 1] = two[:SUB], two[SUB:]
        return found

    keys = jnp.zeros((SUB, LANES), jnp.float32)
    for u in range(NSRC // 8):
        found = tiles_of(u, [b * FOUR + STEP * (m + 1) for b in range(2) for m in range(4)])
        for b in range(2):
            for m in range(4):
                keys = keys + jnp.where(sub == 2 * m + b, found[b * FOUR + STEP * (m + 1)], 0.0)
    key_vmem[...] = keys.astype(jnp.int32)
    copy = pltpu.make_async_copy(key_vmem, key_ref, sem)
    copy.start()
    for acc in accs:
        acc[...] = jnp.zeros_like(acc)
    copy.wait()

    @pl.loop(0, NSRC // 8)
    def _(u):
        found = tiles_of(u, range(2 * FOUR))
        for b in range(2):
            for m in range(4):
                for t in range(NT):
                    row = key_ref[2 * m + b, u * 8 + t] * SUB
                    where = pl.ds(pl.multiple_of(row, SUB), SUB)
                    for half in range(2):
                        first = b * FOUR + STEP * m
                        tile = found[first + 2 * t + half]
                        if t == 0 and half == 0 and m > 0:
                            tile = jnp.where(sub >= 2 * m, tile, found[first + STEP])
                        acc = accs[half * COPIES + (m + t) % COPIES]
                        acc[where, :] = acc[where, :] + tile

    core = lax.axis_index("c")
    for ref, parity in ((keep_ref, core), (send_ref, 1 - core)):
        for high in range(2):
            rows = pl.ds(pl.multiple_of((high * 2 + parity) * SITE_ROWS, SUB), SITE_ROWS)
            for half in range(2):
                total = accs[half * COPIES][rows, :]
                for other in range(1, COPIES):
                    total = total + accs[half * COPIES + other][rows, :]
                ref[high, half] = total


def make_sums(arrived):
    part = jax.ShapeDtypeStruct((2, 2, SITE_ROWS, LANES), jnp.float32)
    return pl.pallas_call(
        sum_kernel,
        in_specs=[pl.BlockSpec(memory_space=pltpu.VMEM)],
        out_specs=[pl.BlockSpec(memory_space=pltpu.VMEM)] * 2,
        out_shape=[part, part],
        scratch_shapes=[
            pltpu.VMEM((SUB, LANES), jnp.int32),
            pltpu.SMEM((SUB, LANES), jnp.int32),
            pltpu.SemaphoreType.DMA,
        ]
        + [pltpu.VMEM((BUCKETS * SUB, LANES), jnp.float32)] * (2 * COPIES),
        compiler_params=pltpu.CompilerParams(vmem_limit_bytes=32 * MIB),
        cost_estimate=pl.CostEstimate(
            flops=NSRC * NT * 2 * BLK, bytes_accessed=2 * MIB, transcendentals=0
        ),
        name="sums",
    )(arrived)


def join_kernel(keep_ref, got_ref, out_ref):
    total = (keep_ref[...] + got_ref[...]).astype(jnp.bfloat16)
    for x in range(4):
        out_ref[x] = total


def make_join(keep, got):
    return pl.pallas_call(
        join_kernel,
        in_specs=[pl.BlockSpec(memory_space=pltpu.VMEM)] * 2,
        out_specs=pl.BlockSpec(memory_space=pltpu.VMEM),
        out_shape=jax.ShapeDtypeStruct((4, 2, 2, SITE_ROWS, LANES), jnp.bfloat16),
        compiler_params=pltpu.CompilerParams(vmem_limit_bytes=32 * MIB),
        name="join",
    )(keep, got)


HALF = LANES // 2
NHI = 32
KPAD = 16


def fit_kernel(site_ref, in_ref, weight_ref, out_ref, scr):
    for k in range(NU_SITE):
        rows = [
            jnp.concatenate([in_ref[x, q, pl.ds(k * SUB, SUB), :] for q in range(4)], axis=0)
            for x in range(4)
        ]
        low = jnp.concatenate([r[:, :HALF] for r in rows], axis=1)
        high = jnp.concatenate([r[:, HALF:] for r in rows], axis=1)
        res = lax.dot_general(
            jnp.concatenate([low, high], axis=0),
            weight_ref[k],
            (((1,), (1,)), ((), ())),
            preferred_element_type=jnp.float32,
        )
        scr[pl.ds(k, NHI, stride=KPAD), :] = jnp.concatenate([res[:NHI], res[NHI:]], axis=1)
    for n in range(NHI):
        out_ref[:, n * LANES : (n + 1) * LANES] = scr[n * KPAD : n * KPAD + NU_SITE, :].astype(
            jnp.bfloat16
        )


def make_fit(site, gathered, fitting):
    return pl.pallas_call(
        fit_kernel,
        grid_spec=pltpu.PrefetchScalarGridSpec(
            num_scalar_prefetch=1,
            grid=(1,),
            in_specs=[
                pl.BlockSpec((4, 4, NU_SITE * SUB, LANES), lambda i, site: (0, 0, 0, 0)),
                pl.BlockSpec((NU_SITE, 64, 256), lambda i, site: (site[0], 0, 0)),
            ],
            out_specs=pl.BlockSpec((NU_SITE, NHI * LANES), lambda i, site: (0, 0)),
            scratch_shapes=[pltpu.VMEM((NHI * KPAD, LANES), jnp.float32)],
        ),
        out_shape=jax.ShapeDtypeStruct((NU_SITE, NHI * LANES), jnp.bfloat16),
        compiler_params=pltpu.CompilerParams(vmem_limit_bytes=32 * MIB),
        name="fit",
    )(site, gathered, fitting)


def local(three_center, pair_mu, pair_site, pair_pos, coeff, fitting):
    pieces = make_pieces(three_center, pair_mu, pair_site, pair_pos, coeff)
    arrived = lax.all_to_all(
        pieces.reshape(NSRC, UNIT // 2, 2, LANES), MAIN, split_axis=0, concat_axis=0, tiled=True
    )
    keep, send = make_sums(arrived.reshape(NSRC * UNIT, LANES))
    got = lax.ppermute(send, "c", [(0, 1), (1, 0)])
    sums = make_join(keep, got)
    gathered = lax.all_to_all(
        sums.reshape(8, 2 * SITE_ROWS, LANES), FIT, split_axis=0, concat_axis=0, tiled=True
    )
    site = lax.axis_index("yl") * 2 + lax.axis_index("c")
    result = make_fit(site.reshape(1), gathered.reshape(4, 4, NU_SITE * SUB, LANES), fitting)
    return result.reshape(1, NU_SITE, 1, 4096)


def solution(mesh):
    fine = Mesh(mesh.devices.reshape(8, 4, 2, 2, 4), ("z", "yh", "yl", "c", "x"))
    mu = ("z", "yh", "yl", "c")
    in_specs = (
        P(mu, None, "x"),
        P(mu, None),
        P(mu, None, None),
        P(mu, None),
        P(),
        P(None, "x", None),
    )
    out_specs = P(mu, None, None, "x")
    return jax.shard_map(local, mesh=fine, in_specs=in_specs, out_specs=out_specs, check_vma=False)
```

```python
import jax
import jax.numpy as jnp
from jax import lax
from jax.experimental import pallas as pl
from jax.experimental.pallas import tpu as pltpu
from jax.sharding import Mesh, PartitionSpec as P

SITES = 4
NU_SITE = 12
NT = 5
BS = 64
NOB = 32
LANES = 128
NSRC = 64
BUCKETS = SITES * NU_SITE
BLK = 1024
SUB = BLK // LANES
PAIR = 2 * SUB
DATA = NT * PAIR
UNIT = DATA + 2
MAIN = ("yl", "z", "yh")
FIT = ("x", "yl")
PART = NOB // 2 * UNIT
MIB = 2**20


def source_index():
    return (lax.axis_index("yl") * 8 + lax.axis_index("z")) * 4 + lax.axis_index("yh")


def piece_kernel(
    mu_hbm, site_hbm, pos_hbm, slab_hbm, coeff_hbm, out_hbm,
    mu, site, pos, slab, coeff, scr, done, small, ins, outs,
):
    def slab_copy(q):
        return pltpu.make_async_copy(
            slab_hbm.at[:, :, pl.ds(q * BLK, BLK)], slab.at[q], ins.at[q]
        )

    def out_copy(part):
        rows = pl.ds(part * PART, PART)
        return pltpu.make_async_copy(done.at[rows, :], out_hbm.at[rows, :], outs.at[part])

    smalls = [
        pltpu.make_async_copy(src, dst, small.at[i])
        for i, (src, dst) in enumerate(
            [(mu_hbm, mu), (coeff_hbm, coeff), (site_hbm, site), (pos_hbm, pos)]
        )
    ]
    for copy in smalls:
        copy.start()
    for q in range(SITES):
        slab_copy(q).start()
    me = source_index()
    shift = me % 4 * 2
    first_lane = me // 8 * 8
    for copy in smalls:
        copy.wait()
    lane = lax.broadcasted_iota(jnp.int32, (NOB, LANES), 1)
    keys = jnp.zeros((NOB, LANES), jnp.int32)
    for t in range(NT):
        keys = jnp.where(lane == first_lane + t, site[0, t] * NU_SITE + pos[0, t], keys)
    for r in range(2):
        scr[pl.ds(DATA + r, NOB, stride=UNIT), :] = keys.astype(jnp.float32)
    mine = []
    for t in range(NT):
        block = mu[0, t]
        both = coeff[:, pl.ds(pl.multiple_of(block // 2 * LANES, LANES), LANES)].astype(jnp.float32)
        mine.append(
            jnp.where(block % 2 == 1, both[:, BS:], both[:, :BS]).astype(jnp.bfloat16)
        )
    for q in range(SITES):
        column, half = divmod(q, 2)
        slab_copy(q).wait()
        for t in range(NT):
            res = jnp.dot(mine[t], slab[q, t], preferred_element_type=jnp.float32)
            for j in range(SUB):
                place = t * PAIR + half * SUB + j - shift
                place = jnp.where(place < 0, place + DATA, place)
                scr[pl.ds(place, NOB, stride=UNIT), :] = res[
                    :, j * LANES : (j + 1) * LANES
                ]
        if half == 1:
            for o in range(2):
                start = (column * 2 + o) * PART
                done[start : start + PART, :] = scr[o * PART : (o + 1) * PART, :].astype(
                    jnp.bfloat16
                )
                out_copy(column * 2 + o).start()
    for part in range(4):
        out_copy(part).wait()


def make_pieces(three_center, pair_mu, pair_site, pair_pos, coeff):
    return pl.pallas_call(
        piece_kernel,
        in_specs=[pl.BlockSpec(memory_space=pl.ANY)] * 5,
        out_specs=pl.BlockSpec(memory_space=pl.ANY),
        out_shape=jax.ShapeDtypeStruct((4 * PART, LANES), jnp.bfloat16),
        scratch_shapes=[
            pltpu.SMEM((1, NT), jnp.int32),
            pltpu.SMEM((1, NT), jnp.int32),
            pltpu.SMEM((1, NT), jnp.int32),
            pltpu.VMEM((SITES, NT, BS, BLK), jnp.bfloat16),
            pltpu.VMEM((NOB, 3072), jnp.bfloat16),
            pltpu.VMEM((NOB * UNIT, LANES), jnp.float32),
            pltpu.VMEM((4 * PART, LANES), jnp.bfloat16),
            pltpu.SemaphoreType.DMA((4,)),
            pltpu.SemaphoreType.DMA((SITES,)),
            pltpu.SemaphoreType.DMA((SITES,)),
        ],
        compiler_params=pltpu.CompilerParams(vmem_limit_bytes=58 * MIB),
        cost_estimate=pl.CostEstimate(
            flops=2 * NT * BS * NOB * 4096, bytes_accessed=4 * MIB, transcendentals=0
        ),
        name="pieces",
    )(pair_mu, pair_site[:, :, 0], pair_pos, three_center, coeff.T)


COPIES = 2
STEP = 2 * NT
FOUR = 4 * UNIT // SUB
SITE_ROWS = NU_SITE * SUB


def sum_kernel(in_ref, keep_ref, send_ref, key_vmem, key_ref, sem, *accs):
    sub = lax.broadcasted_iota(jnp.int32, (SUB, LANES), 0)

    def tiles_of(two_blocks, wanted):
        found = {}
        for pair in sorted({tile // 2 for tile in wanted}):
            start = pl.multiple_of((two_blocks * FOUR + pair) * 2 * SUB, 2 * SUB)
            two = in_ref[pl.ds(start, 2 * SUB), :].astype(jnp.float32)
            found[pair * 2], found[pair * 2 + 1] = two[:SUB], two[SUB:]
        return found

    keys = jnp.zeros((SUB, LANES), jnp.float32)
    for u in range(NSRC // 8):
        found = tiles_of(u, [b * FOUR + STEP * (m + 1) for b in range(2) for m in range(4)])
        for b in range(2):
            for m in range(4):
                keys = keys + jnp.where(sub == 2 * m + b, found[b * FOUR + STEP * (m + 1)], 0.0)
    key_vmem[...] = keys.astype(jnp.int32)
    copy = pltpu.make_async_copy(key_vmem, key_ref, sem)
    copy.start()
    for acc in accs:
        acc[...] = jnp.zeros_like(acc)
    copy.wait()

    @pl.loop(0, NSRC // 8)
    def _(u):
        found = tiles_of(u, range(2 * FOUR))
        for b in range(2):
            for m in range(4):
                for t in range(NT):
                    row = key_ref[2 * m + b, u * 8 + t] * SUB
                    where = pl.ds(pl.multiple_of(row, SUB), SUB)
                    for half in range(2):
                        first = b * FOUR + STEP * m
                        tile = found[first + 2 * t + half]
                        if t == 0 and half == 0 and m > 0:
                            tile = jnp.where(sub >= 2 * m, tile, found[first + STEP])
                        acc = accs[half * COPIES + (m + t) % COPIES]
                        acc[where, :] = acc[where, :] + tile

    core = lax.axis_index("c")
    for ref, parity in ((keep_ref, core), (send_ref, 1 - core)):
        for high in range(2):
            rows = pl.ds(pl.multiple_of((high * 2 + parity) * SITE_ROWS, SUB), SITE_ROWS)
            for half in range(2):
                total = accs[half * COPIES][rows, :]
                for other in range(1, COPIES):
                    total = total + accs[half * COPIES + other][rows, :]
                ref[high, half] = total


def make_sums(arrived):
    part = jax.ShapeDtypeStruct((2, 2, SITE_ROWS, LANES), jnp.float32)
    return pl.pallas_call(
        sum_kernel,
        in_specs=[pl.BlockSpec(memory_space=pltpu.VMEM)],
        out_specs=[pl.BlockSpec(memory_space=pltpu.VMEM)] * 2,
        out_shape=[part, part],
        scratch_shapes=[
            pltpu.VMEM((SUB, LANES), jnp.int32),
            pltpu.SMEM((SUB, LANES), jnp.int32),
            pltpu.SemaphoreType.DMA,
        ]
        + [pltpu.VMEM((BUCKETS * SUB, LANES), jnp.float32)] * (2 * COPIES),
        compiler_params=pltpu.CompilerParams(vmem_limit_bytes=32 * MIB),
        cost_estimate=pl.CostEstimate(
            flops=NSRC * NT * 2 * BLK, bytes_accessed=2 * MIB, transcendentals=0
        ),
        name="sums",
    )(arrived)


def join_kernel(keep_ref, both_ref, out_ref):
    total = (keep_ref[...] + both_ref[1 - lax.axis_index("c")]).astype(jnp.bfloat16)
    for x in range(4):
        out_ref[x] = total


def make_join(keep, both):
    return pl.pallas_call(
        join_kernel,
        in_specs=[pl.BlockSpec(memory_space=pltpu.VMEM)] * 2,
        out_specs=pl.BlockSpec(memory_space=pltpu.VMEM),
        out_shape=jax.ShapeDtypeStruct((4, 2, 2, SITE_ROWS, LANES), jnp.bfloat16),
        compiler_params=pltpu.CompilerParams(vmem_limit_bytes=32 * MIB),
        name="join",
    )(keep, both)


HALF = LANES // 2
NHI = 32
KPAD = 16


def fit_kernel(site_ref, in_ref, weight_ref, out_ref, scr):
    for k in range(NU_SITE):
        rows = [
            jnp.concatenate([in_ref[x, q, pl.ds(k * SUB, SUB), :] for q in range(4)], axis=0)
            for x in range(4)
        ]
        low = jnp.concatenate([r[:, :HALF] for r in rows], axis=1)
        high = jnp.concatenate([r[:, HALF:] for r in rows], axis=1)
        res = lax.dot_general(
            jnp.concatenate([low, high], axis=0),
            weight_ref[k],
            (((1,), (1,)), ((), ())),
            preferred_element_type=jnp.float32,
        )
        scr[pl.ds(k, NHI, stride=KPAD), :] = jnp.concatenate([res[:NHI], res[NHI:]], axis=1)
    for n in range(NHI):
        out_ref[:, n * LANES : (n + 1) * LANES] = scr[n * KPAD : n * KPAD + NU_SITE, :].astype(
            jnp.bfloat16
        )


def make_fit(site, gathered, fitting):
    return pl.pallas_call(
        fit_kernel,
        grid_spec=pltpu.PrefetchScalarGridSpec(
            num_scalar_prefetch=1,
            grid=(1,),
            in_specs=[
                pl.BlockSpec((4, 4, NU_SITE * SUB, LANES), lambda i, site: (0, 0, 0, 0)),
                pl.BlockSpec((NU_SITE, 64, 256), lambda i, site: (site[0], 0, 0)),
            ],
            out_specs=pl.BlockSpec((NU_SITE, NHI * LANES), lambda i, site: (0, 0)),
            scratch_shapes=[pltpu.VMEM((NHI * KPAD, LANES), jnp.float32)],
        ),
        out_shape=jax.ShapeDtypeStruct((NU_SITE, NHI * LANES), jnp.bfloat16),
        compiler_params=pltpu.CompilerParams(vmem_limit_bytes=32 * MIB),
        name="fit",
    )(site, gathered, fitting)


def local(three_center, pair_mu, pair_site, pair_pos, coeff, fitting):
    pieces = make_pieces(three_center, pair_mu, pair_site, pair_pos, coeff)
    arrived = lax.all_to_all(
        pieces.reshape(NSRC, UNIT // 2, 2, LANES), MAIN, split_axis=0, concat_axis=0, tiled=True
    )
    keep, send = make_sums(arrived.reshape(NSRC * UNIT, LANES))
    both = lax.all_gather(send, "c", axis=0)
    sums = make_join(keep, both)
    gathered = lax.all_to_all(
        sums.reshape(8, 2 * SITE_ROWS, LANES), FIT, split_axis=0, concat_axis=0, tiled=True
    )
    site = lax.axis_index("yl") * 2 + lax.axis_index("c")
    result = make_fit(site.reshape(1), gathered.reshape(4, 4, NU_SITE * SUB, LANES), fitting)
    return result.reshape(1, NU_SITE, 1, 4096)


def solution(mesh):
    fine = Mesh(mesh.devices.reshape(8, 4, 2, 2, 4), ("z", "yh", "yl", "c", "x"))
    mu = ("z", "yh", "yl", "c")
    in_specs = (
        P(mu, None, "x"),
        P(mu, None),
        P(mu, None, None),
        P(mu, None),
        P(),
        P(None, "x", None),
    )
    out_specs = P(mu, None, None, "x")
    return jax.shard_map(local, mesh=fine, in_specs=in_specs, out_specs=out_specs, check_vma=False)
```

```python
import jax
import jax.numpy as jnp
from jax import lax
from jax.experimental import pallas as pl
from jax.experimental.pallas import tpu as pltpu
from jax.sharding import Mesh, PartitionSpec as P

SITES = 4
NU_SITE = 12
NT = 5
BS = 64
NOB = 32
LANES = 128
NSRC = 64
BUCKETS = SITES * NU_SITE
BLK = 1024
SUB = BLK // LANES
PAIR = 2 * SUB
DATA = NT * PAIR
UNIT = DATA + 2
MAIN = ("yl", "z", "yh")
FIT = ("x", "yl")
MIB = 2**20


def source_index():
    return (lax.axis_index("yl") * 8 + lax.axis_index("z")) * 4 + lax.axis_index("yh")


def piece_kernel(
    mu_hbm, site_hbm, pos_hbm, slab_hbm, coeff_hbm, out_ref,
    mu, site, pos, slab, coeff, scr, small, ins,
):
    def slab_copy(q):
        return pltpu.make_async_copy(
            slab_hbm.at[:, :, pl.ds(q * BLK, BLK)], slab.at[q], ins.at[q]
        )

    smalls = [
        pltpu.make_async_copy(src, dst, small.at[i])
        for i, (src, dst) in enumerate(
            [(mu_hbm, mu), (coeff_hbm, coeff), (site_hbm, site), (pos_hbm, pos)]
        )
    ]
    for copy in smalls:
        copy.start()
    for q in range(SITES):
        slab_copy(q).start()
    me = source_index()
    shift = me % 4 * 2
    first_lane = me // 8 * 8
    for copy in smalls:
        copy.wait()
    lane = lax.broadcasted_iota(jnp.int32, (NOB, LANES), 1)
    keys = jnp.zeros((NOB, LANES), jnp.int32)
    for t in range(NT):
        keys = jnp.where(lane == first_lane + t, site[0, t] * NU_SITE + pos[0, t], keys)
    for r in range(2):
        scr[pl.ds(DATA + r, NOB, stride=UNIT), :] = keys.astype(jnp.float32)
    mine = []
    for t in range(NT):
        block = mu[0, t]
        both = coeff[:, pl.ds(pl.multiple_of(block // 2 * LANES, LANES), LANES)].astype(jnp.float32)
        mine.append(
            jnp.where(block % 2 == 1, both[:, BS:], both[:, :BS]).astype(jnp.bfloat16)
        )
    for q in range(SITES):
        column, half = divmod(q, 2)
        slab_copy(q).wait()
        for t in range(NT):
            res = jnp.dot(mine[t], slab[q, t], preferred_element_type=jnp.float32)
            for j in range(SUB):
                place = t * PAIR + half * SUB + j - shift
                place = jnp.where(place < 0, place + DATA, place)
                scr[pl.ds(place, NOB, stride=UNIT), :] = res[
                    :, j * LANES : (j + 1) * LANES
                ]
        if half == 1:
            start = column * NOB * UNIT
            out_ref[start : start + NOB * UNIT, :] = scr[...].astype(jnp.bfloat16)


def make_pieces(three_center, pair_mu, pair_site, pair_pos, coeff):
    return pl.pallas_call(
        piece_kernel,
        in_specs=[pl.BlockSpec(memory_space=pltpu.HBM)] * 5,
        out_specs=pl.BlockSpec(memory_space=pltpu.VMEM),
        out_shape=pltpu.VMEM((2 * NOB * UNIT, LANES), jnp.bfloat16),
        scratch_shapes=[
            pltpu.SMEM((1, NT), jnp.int32),
            pltpu.SMEM((1, NT), jnp.int32),
            pltpu.SMEM((1, NT), jnp.int32),
            pltpu.VMEM((SITES, NT, BS, BLK), jnp.bfloat16),
            pltpu.VMEM((NOB, 3072), jnp.bfloat16),
            pltpu.VMEM((NOB * UNIT, LANES), jnp.float32),
            pltpu.SemaphoreType.DMA((4,)),
            pltpu.SemaphoreType.DMA((SITES,)),
        ],
        compiler_params=pltpu.CompilerParams(vmem_limit_bytes=58 * MIB),
        cost_estimate=pl.CostEstimate(
            flops=2 * NT * BS * NOB * 4096, bytes_accessed=4 * MIB, transcendentals=0
        ),
        name="pieces",
    )(pair_mu, pair_site[:, :, 0], pair_pos, three_center, coeff.T)


COPIES = 2
STEP = 2 * NT
FOUR = 4 * UNIT // SUB
SITE_ROWS = NU_SITE * SUB


def sum_kernel(in_ref, keep_ref, send_ref, key_vmem, key_ref, sem, *accs):
    sub = lax.broadcasted_iota(jnp.int32, (SUB, LANES), 0)

    def tiles_of(two_blocks, wanted):
        found = {}
        for pair in sorted({tile // 2 for tile in wanted}):
            start = pl.multiple_of((two_blocks * FOUR + pair) * 2 * SUB, 2 * SUB)
            two = in_ref[pl.ds(start, 2 * SUB), :].astype(jnp.float32)
            found[pair * 2], found[pair * 2 + 1] = two[:SUB], two[SUB:]
        return found

    keys = jnp.zeros((SUB, LANES), jnp.float32)
    for u in range(NSRC // 8):
        found = tiles_of(u, [b * FOUR + STEP * (m + 1) for b in range(2) for m in range(4)])
        for b in range(2):
            for m in range(4):
                keys = keys + jnp.where(sub == 2 * m + b, found[b * FOUR + STEP * (m + 1)], 0.0)
    key_vmem[...] = keys.astype(jnp.int32)
    copy = pltpu.make_async_copy(key_vmem, key_ref, sem)
    copy.start()
    for acc in accs:
        acc[...] = jnp.zeros_like(acc)
    copy.wait()

    @pl.loop(0, NSRC // 8)
    def _(u):
        found = tiles_of(u, range(2 * FOUR))
        for b in range(2):
            for m in range(4):
                for t in range(NT):
                    row = key_ref[2 * m + b, u * 8 + t] * SUB
                    where = pl.ds(pl.multiple_of(row, SUB), SUB)
                    for half in range(2):
                        first = b * FOUR + STEP * m
                        tile = found[first + 2 * t + half]
                        if t == 0 and half == 0 and m > 0:
                            tile = jnp.where(sub >= 2 * m, tile, found[first + STEP])
                        acc = accs[half * COPIES + (m + t) % COPIES]
                        acc[where, :] = acc[where, :] + tile

    core = lax.axis_index("c")
    for ref, parity in ((keep_ref, core), (send_ref, 1 - core)):
        for high in range(2):
            rows = pl.ds(pl.multiple_of((high * 2 + parity) * SITE_ROWS, SUB), SITE_ROWS)
            for half in range(2):
                total = accs[half * COPIES][rows, :]
                for other in range(1, COPIES):
                    total = total + accs[half * COPIES + other][rows, :]
                ref[high, half] = total


def make_sums(arrived):
    part = jax.ShapeDtypeStruct((2, 2, SITE_ROWS, LANES), jnp.float32)
    return pl.pallas_call(
        sum_kernel,
        in_specs=[pl.BlockSpec(memory_space=pltpu.VMEM)],
        out_specs=[pl.BlockSpec(memory_space=pltpu.VMEM)] * 2,
        out_shape=[part, part],
        scratch_shapes=[
            pltpu.VMEM((SUB, LANES), jnp.int32),
            pltpu.SMEM((SUB, LANES), jnp.int32),
            pltpu.SemaphoreType.DMA,
        ]
        + [pltpu.VMEM((BUCKETS * SUB, LANES), jnp.float32)] * (2 * COPIES),
        compiler_params=pltpu.CompilerParams(vmem_limit_bytes=32 * MIB),
        cost_estimate=pl.CostEstimate(
            flops=NSRC * NT * 2 * BLK, bytes_accessed=2 * MIB, transcendentals=0
        ),
        name="sums",
    )(arrived)


def join_kernel(keep_ref, both_ref, out_ref):
    total = (keep_ref[...] + both_ref[1 - lax.axis_index("c")]).astype(jnp.bfloat16)
    for x in range(4):
        out_ref[x] = total


def make_join(keep, both):
    return pl.pallas_call(
        join_kernel,
        in_specs=[pl.BlockSpec(memory_space=pltpu.VMEM)] * 2,
        out_specs=pl.BlockSpec(memory_space=pltpu.VMEM),
        out_shape=jax.ShapeDtypeStruct((4, 2, 2, SITE_ROWS, LANES), jnp.bfloat16),
        compiler_params=pltpu.CompilerParams(vmem_limit_bytes=32 * MIB),
        name="join",
    )(keep, both)


HALF = LANES // 2
NHI = 32
KPAD = 16


def fit_kernel(site_ref, in_ref, weight_ref, out_ref, scr):
    for k in range(NU_SITE):
        rows = [
            jnp.concatenate([in_ref[x, q, pl.ds(k * SUB, SUB), :] for q in range(4)], axis=0)
            for x in range(4)
        ]
        low = jnp.concatenate([r[:, :HALF] for r in rows], axis=1)
        high = jnp.concatenate([r[:, HALF:] for r in rows], axis=1)
        res = lax.dot_general(
            jnp.concatenate([low, high], axis=0),
            weight_ref[k],
            (((1,), (1,)), ((), ())),
            preferred_element_type=jnp.float32,
        )
        scr[pl.ds(k, NHI, stride=KPAD), :] = jnp.concatenate([res[:NHI], res[NHI:]], axis=1)
    for n in range(NHI):
        out_ref[:, n * LANES : (n + 1) * LANES] = scr[n * KPAD : n * KPAD + NU_SITE, :].astype(
            jnp.bfloat16
        )


def make_fit(site, gathered, fitting):
    return pl.pallas_call(
        fit_kernel,
        grid_spec=pltpu.PrefetchScalarGridSpec(
            num_scalar_prefetch=1,
            grid=(1,),
            in_specs=[
                pl.BlockSpec((4, 4, NU_SITE * SUB, LANES), lambda i, site: (0, 0, 0, 0)),
                pl.BlockSpec((NU_SITE, 64, 256), lambda i, site: (site[0], 0, 0)),
            ],
            out_specs=pl.BlockSpec((NU_SITE, NHI * LANES), lambda i, site: (0, 0)),
            scratch_shapes=[pltpu.VMEM((NHI * KPAD, LANES), jnp.float32)],
        ),
        out_shape=jax.ShapeDtypeStruct((NU_SITE, NHI * LANES), jnp.bfloat16),
        compiler_params=pltpu.CompilerParams(vmem_limit_bytes=32 * MIB),
        name="fit",
    )(site, gathered, fitting)


def local(three_center, pair_mu, pair_site, pair_pos, coeff, fitting):
    pieces = make_pieces(three_center, pair_mu, pair_site, pair_pos, coeff)
    arrived = lax.all_to_all(
        pieces.reshape(NSRC, UNIT // 2, 2, LANES), MAIN, split_axis=0, concat_axis=0, tiled=True
    )
    keep, send = make_sums(arrived.reshape(NSRC * UNIT, LANES))
    both = lax.all_gather(send, "c", axis=0)
    sums = make_join(keep, both)
    gathered = lax.all_to_all(
        sums.reshape(8, 2 * SITE_ROWS, LANES), FIT, split_axis=0, concat_axis=0, tiled=True
    )
    site = lax.axis_index("yl") * 2 + lax.axis_index("c")
    result = make_fit(site.reshape(1), gathered.reshape(4, 4, NU_SITE * SUB, LANES), fitting)
    return result.reshape(1, NU_SITE, 1, 4096)


def solution(mesh):
    fine = Mesh(mesh.devices.reshape(8, 4, 2, 2, 4), ("z", "yh", "yl", "c", "x"))
    mu = ("z", "yh", "yl", "c")
    in_specs = (
        P(mu, None, "x"),
        P(mu, None),
        P(mu, None, None),
        P(mu, None),
        P(),
        P(None, "x", None),
    )
    out_specs = P(mu, None, None, "x")
    return jax.shard_map(local, mesh=fine, in_specs=in_specs, out_specs=out_specs, check_vma=False)
```

```python
import jax
import jax.numpy as jnp
from jax import lax
from jax.experimental import pallas as pl
from jax.experimental.pallas import tpu as pltpu
from jax.sharding import Mesh, PartitionSpec as P

SITES = 4
NU_SITE = 12
NT = 5
BS = 64
NOB = 32
LANES = 128
NSRC = 64
BUCKETS = SITES * NU_SITE
BLK = 1024
SUB = BLK // LANES
PAIR = 2 * SUB
DATA = NT * PAIR
UNIT = DATA + 2
MAIN = ("yl", "z", "yh")
FIT = ("x", "yl")
MIB = 2**20


def source_index():
    return (lax.axis_index("yl") * 8 + lax.axis_index("z")) * 4 + lax.axis_index("yh")


def piece_kernel(
    mu_hbm, site_hbm, pos_hbm, slab_hbm, coeff_hbm, out_ref,
    mu, site, pos, slab, coeff, scr, small, ins,
):
    def slab_copy(q):
        return pltpu.make_async_copy(
            slab_hbm.at[:, :, pl.ds(q * BLK, BLK)], slab.at[q], ins.at[q]
        )

    smalls = [
        pltpu.make_async_copy(src, dst, small.at[i])
        for i, (src, dst) in enumerate(
            [(mu_hbm, mu), (coeff_hbm, coeff), (site_hbm, site), (pos_hbm, pos)]
        )
    ]
    for copy in smalls:
        copy.start()
    for q in range(SITES):
        slab_copy(q).start()
    me = source_index()
    shift = me % 4 * 2
    first_lane = me // 8 * 8
    for copy in smalls:
        copy.wait()
    lane = lax.broadcasted_iota(jnp.int32, (NOB, LANES), 1)
    keys = jnp.zeros((NOB, LANES), jnp.int32)
    for t in range(NT):
        keys = jnp.where(lane == first_lane + t, site[0, t] * NU_SITE + pos[0, t], keys)
    for r in range(2):
        scr[pl.ds(DATA + r, NOB, stride=UNIT), :] = keys.astype(jnp.float32)
    mine = []
    for t in range(NT):
        block = mu[0, t]
        both = coeff[:, pl.ds(pl.multiple_of(block // 2 * LANES, LANES), LANES)].astype(jnp.float32)
        mine.append(
            jnp.where(block % 2 == 1, both[:, BS:], both[:, :BS]).astype(jnp.bfloat16)
        )
    for q in range(SITES):
        column, half = divmod(q, 2)
        slab_copy(q).wait()
        for t in range(NT):
            res = jnp.dot(mine[t], slab[q, t], preferred_element_type=jnp.float32)
            for j in range(SUB):
                place = t * PAIR + half * SUB + j - shift
                place = jnp.where(place < 0, place + DATA, place)
                scr[pl.ds(place, NOB, stride=UNIT), :] = res[
                    :, j * LANES : (j + 1) * LANES
                ]
        if half == 1:
            start = column * NOB * UNIT
            out_ref[start : start + NOB * UNIT, :] = scr[...].astype(jnp.bfloat16)


def make_pieces(three_center, pair_mu, pair_site, pair_pos, coeff):
    return pl.pallas_call(
        piece_kernel,
        in_specs=[pl.BlockSpec(memory_space=pltpu.HBM)] * 5,
        out_specs=pl.BlockSpec(memory_space=pltpu.VMEM),
        out_shape=pltpu.VMEM((2 * NOB * UNIT, LANES), jnp.bfloat16),
        scratch_shapes=[
            pltpu.SMEM((1, NT), jnp.int32),
            pltpu.SMEM((1, NT), jnp.int32),
            pltpu.SMEM((1, NT), jnp.int32),
            pltpu.VMEM((SITES, NT, BS, BLK), jnp.bfloat16),
            pltpu.VMEM((NOB, 3072), jnp.bfloat16),
            pltpu.VMEM((NOB * UNIT, LANES), jnp.float32),
            pltpu.SemaphoreType.DMA((4,)),
            pltpu.SemaphoreType.DMA((SITES,)),
        ],
        compiler_params=pltpu.CompilerParams(vmem_limit_bytes=58 * MIB),
        cost_estimate=pl.CostEstimate(
            flops=2 * NT * BS * NOB * 4096, bytes_accessed=4 * MIB, transcendentals=0
        ),
        name="pieces",
    )(pair_mu, pair_site[:, :, 0], pair_pos, three_center, coeff.T)


COPIES = 2
STEP = 2 * NT
FOUR = 4 * UNIT // SUB
SITE_ROWS = NU_SITE * SUB


def sum_kernel(in_ref, keep_ref, send_ref, key_vmem, key_ref, sem, *accs):
    sub = lax.broadcasted_iota(jnp.int32, (SUB, LANES), 0)

    def tiles_of(two_blocks, wanted):
        found = {}
        for pair in sorted({tile // 2 for tile in wanted}):
            start = pl.multiple_of((two_blocks * FOUR + pair) * 2 * SUB, 2 * SUB)
            two = in_ref[pl.ds(start, 2 * SUB), :].astype(jnp.float32)
            found[pair * 2], found[pair * 2 + 1] = two[:SUB], two[SUB:]
        return found

    keys = jnp.zeros((SUB, LANES), jnp.float32)
    for u in range(NSRC // 8):
        found = tiles_of(u, [b * FOUR + STEP * (m + 1) for b in range(2) for m in range(4)])
        for b in range(2):
            for m in range(4):
                keys = keys + jnp.where(sub == 2 * m + b, found[b * FOUR + STEP * (m + 1)], 0.0)
    key_vmem[...] = keys.astype(jnp.int32)
    copy = pltpu.make_async_copy(key_vmem, key_ref, sem)
    copy.start()
    for acc in accs:
        acc[...] = jnp.zeros_like(acc)
    copy.wait()

    @pl.loop(0, NSRC // 8)
    def _(u):
        found = tiles_of(u, range(2 * FOUR))
        for b in range(2):
            for m in range(4):
                for t in range(NT):
                    row = key_ref[2 * m + b, u * 8 + t] * SUB
                    where = pl.ds(pl.multiple_of(row, SUB), SUB)
                    for half in range(2):
                        first = b * FOUR + STEP * m
                        tile = found[first + 2 * t + half]
                        if t == 0 and half == 0 and m > 0:
                            tile = jnp.where(sub >= 2 * m, tile, found[first + STEP])
                        acc = accs[half * COPIES + (m + t) % COPIES]
                        acc[where, :] = acc[where, :] + tile

    core = lax.axis_index("c")
    for ref, parity in ((keep_ref, core), (send_ref, 1 - core)):
        for high in range(2):
            rows = pl.ds(pl.multiple_of((high * 2 + parity) * SITE_ROWS, SUB), SITE_ROWS)
            for half in range(2):
                total = accs[half * COPIES][rows, :]
                for other in range(1, COPIES):
                    total = total + accs[half * COPIES + other][rows, :]
                ref[high, half] = total


def make_sums(arrived):
    part = jax.ShapeDtypeStruct((2, 2, SITE_ROWS, LANES), jnp.float32)
    return pl.pallas_call(
        sum_kernel,
        in_specs=[pl.BlockSpec(memory_space=pltpu.VMEM)],
        out_specs=[pl.BlockSpec(memory_space=pltpu.VMEM)] * 2,
        out_shape=[part, part],
        scratch_shapes=[
            pltpu.VMEM((SUB, LANES), jnp.int32),
            pltpu.SMEM((SUB, LANES), jnp.int32),
            pltpu.SemaphoreType.DMA,
        ]
        + [pltpu.VMEM((BUCKETS * SUB, LANES), jnp.float32)] * (2 * COPIES),
        compiler_params=pltpu.CompilerParams(vmem_limit_bytes=32 * MIB),
        cost_estimate=pl.CostEstimate(
            flops=NSRC * NT * 2 * BLK, bytes_accessed=2 * MIB, transcendentals=0
        ),
        name="sums",
    )(arrived)


def join_kernel(keep_ref, both_ref, out_ref):
    total = (keep_ref[...] + both_ref[1 - lax.axis_index("c")]).astype(jnp.bfloat16)
    for x in range(4):
        out_ref[x] = total


def make_join(keep, both):
    return pl.pallas_call(
        join_kernel,
        in_specs=[pl.BlockSpec(memory_space=pltpu.VMEM)] * 2,
        out_specs=pl.BlockSpec(memory_space=pltpu.VMEM),
        out_shape=jax.ShapeDtypeStruct((4, 2, 2, SITE_ROWS, LANES), jnp.bfloat16),
        compiler_params=pltpu.CompilerParams(vmem_limit_bytes=32 * MIB),
        name="join",
    )(keep, both)


HALF = LANES // 2
NHI = 32
KPAD = 16


def fit_kernel(in_ref, weight_ref, out_ref, scr):
    site = lax.axis_index("yl") * 2 + lax.axis_index("c")
    for k in range(NU_SITE):
        rows = [
            jnp.concatenate([in_ref[x, q, pl.ds(k * SUB, SUB), :] for q in range(4)], axis=0)
            for x in range(4)
        ]
        low = jnp.concatenate([r[:, :HALF] for r in rows], axis=1)
        high = jnp.concatenate([r[:, HALF:] for r in rows], axis=1)
        res = lax.dot_general(
            jnp.concatenate([low, high], axis=0),
            weight_ref[site * NU_SITE + k],
            (((1,), (1,)), ((), ())),
            preferred_element_type=jnp.float32,
        )
        scr[pl.ds(k, NHI, stride=KPAD), :] = jnp.concatenate([res[:NHI], res[NHI:]], axis=1)
    for n in range(NHI):
        out_ref[:, n * LANES : (n + 1) * LANES] = scr[n * KPAD : n * KPAD + NU_SITE, :].astype(
            jnp.bfloat16
        )


def make_fit(gathered, fitting):
    return pl.pallas_call(
        fit_kernel,
        in_specs=[pl.BlockSpec(memory_space=pltpu.VMEM)] * 2,
        out_specs=pl.BlockSpec(memory_space=pltpu.VMEM),
        out_shape=jax.ShapeDtypeStruct((NU_SITE, NHI * LANES), jnp.bfloat16),
        scratch_shapes=[pltpu.VMEM((NHI * KPAD, LANES), jnp.float32)],
        compiler_params=pltpu.CompilerParams(vmem_limit_bytes=32 * MIB),
        name="fit",
    )(gathered, fitting)


def local(three_center, pair_mu, pair_site, pair_pos, coeff, fitting):
    pieces = make_pieces(three_center, pair_mu, pair_site, pair_pos, coeff)
    arrived = lax.all_to_all(
        pieces.reshape(NSRC, UNIT // 2, 2, LANES), MAIN, split_axis=0, concat_axis=0, tiled=True
    )
    keep, send = make_sums(arrived.reshape(NSRC * UNIT, LANES))
    both = lax.all_gather(send, "c", axis=0)
    sums = make_join(keep, both)
    gathered = lax.all_to_all(
        sums.reshape(8, 2 * SITE_ROWS, LANES), FIT, split_axis=0, concat_axis=0, tiled=True
    )
    result = make_fit(gathered.reshape(4, 4, NU_SITE * SUB, LANES), fitting)
    return result.reshape(1, NU_SITE, 1, 4096)


def solution(mesh):
    fine = Mesh(mesh.devices.reshape(8, 4, 2, 2, 4), ("z", "yh", "yl", "c", "x"))
    mu = ("z", "yh", "yl", "c")
    in_specs = (
        P(mu, None, "x"),
        P(mu, None),
        P(mu, None, None),
        P(mu, None),
        P(),
        P(None, "x", None),
    )
    out_specs = P(mu, None, None, "x")
    return jax.shard_map(local, mesh=fine, in_specs=in_specs, out_specs=out_specs, check_vma=False)
```

```python
import jax
import jax.numpy as jnp
from jax import lax
from jax.experimental import pallas as pl
from jax.experimental.pallas import tpu as pltpu
from jax.sharding import Mesh, PartitionSpec as P

SITES = 4
NU_SITE = 12
NT = 5
BS = 64
NOB = 32
LANES = 128
NSRC = 64
BUCKETS = SITES * NU_SITE
BLK = 1024
SUB = BLK // LANES
PAIR = 2 * SUB
DATA = NT * PAIR
UNIT = DATA + 2
MAIN = ("yl", "z", "yh")
FIT = ("x", "yl")
MIB = 2**20


def source_index():
    return (lax.axis_index("yl") * 8 + lax.axis_index("z")) * 4 + lax.axis_index("yh")


def piece_kernel(
    mu_hbm, site_hbm, pos_hbm, slab_hbm, coeff_hbm, out_ref,
    mu, site, pos, slab, coeff, scr, small, ins,
):
    def slab_copy(q):
        return pltpu.make_async_copy(
            slab_hbm.at[:, :, pl.ds(q * BLK, BLK)], slab.at[q], ins.at[q]
        )

    smalls = [
        pltpu.make_async_copy(src, dst, small.at[i])
        for i, (src, dst) in enumerate(
            [(mu_hbm, mu), (coeff_hbm, coeff), (site_hbm, site), (pos_hbm, pos)]
        )
    ]
    for copy in smalls:
        copy.start()
    for q in range(SITES):
        slab_copy(q).start()
    me = source_index()
    shift = me % 4 * 2
    first_lane = me // 8 * 8
    for copy in smalls:
        copy.wait()
    lane = lax.broadcasted_iota(jnp.int32, (NOB, LANES), 1)
    keys = jnp.zeros((NOB, LANES), jnp.int32)
    for t in range(NT):
        keys = jnp.where(lane == first_lane + t, site[0, t] * NU_SITE + pos[0, t], keys)
    for r in range(2):
        scr[pl.ds(DATA + r, NOB, stride=UNIT), :] = keys.astype(jnp.float32)
    mine = []
    for t in range(NT):
        block = mu[0, t]
        both = coeff[:, pl.ds(pl.multiple_of(block // 2 * LANES, LANES), LANES)].astype(jnp.float32)
        mine.append(
            jnp.where(block % 2 == 1, both[:, BS:], both[:, :BS]).astype(jnp.bfloat16)
        )
    for q in range(SITES):
        column, half = divmod(q, 2)
        slab_copy(q).wait()
        for t in range(NT):
            res = jnp.dot(mine[t], slab[q, t], preferred_element_type=jnp.float32)
            for j in range(SUB):
                place = t * PAIR + half * SUB + j - shift
                place = jnp.where(place < 0, place + DATA, place)
                scr[pl.ds(place, NOB, stride=UNIT), :] = res[
                    :, j * LANES : (j + 1) * LANES
                ]
        if half == 1:
            start = column * NOB * UNIT
            out_ref[start : start + NOB * UNIT, :] = scr[...].astype(jnp.bfloat16)


def make_pieces(three_center, pair_mu, pair_site, pair_pos, coeff):
    return pl.pallas_call(
        piece_kernel,
        in_specs=[pl.BlockSpec(memory_space=pltpu.HBM)] * 5,
        out_specs=pl.BlockSpec(memory_space=pltpu.VMEM),
        out_shape=pltpu.VMEM((2 * NOB * UNIT, LANES), jnp.bfloat16),
        scratch_shapes=[
            pltpu.SMEM((1, NT), jnp.int32),
            pltpu.SMEM((1, NT), jnp.int32),
            pltpu.SMEM((1, NT), jnp.int32),
            pltpu.VMEM((SITES, NT, BS, BLK), jnp.bfloat16),
            pltpu.VMEM((NOB, 3072), jnp.bfloat16),
            pltpu.VMEM((NOB * UNIT, LANES), jnp.float32),
            pltpu.SemaphoreType.DMA((4,)),
            pltpu.SemaphoreType.DMA((SITES,)),
        ],
        compiler_params=pltpu.CompilerParams(vmem_limit_bytes=58 * MIB),
        cost_estimate=pl.CostEstimate(
            flops=2 * NT * BS * NOB * 4096, bytes_accessed=4 * MIB, transcendentals=0
        ),
        name="pieces",
    )(pair_mu, pair_site[:, :, 0], pair_pos, three_center, coeff.T)


COPIES = 2
STEP = 2 * NT
FOUR = 4 * UNIT // SUB
SITE_ROWS = NU_SITE * SUB


def sum_kernel(in_ref, keep_ref, send_ref, key_vmem, key_ref, sem, *accs):
    sub = lax.broadcasted_iota(jnp.int32, (SUB, LANES), 0)

    def tiles_of(two_blocks, wanted):
        found = {}
        for pair in sorted({tile // 2 for tile in wanted}):
            start = pl.multiple_of((two_blocks * FOUR + pair) * 2 * SUB, 2 * SUB)
            two = in_ref[pl.ds(start, 2 * SUB), :].astype(jnp.float32)
            found[pair * 2], found[pair * 2 + 1] = two[:SUB], two[SUB:]
        return found

    keys = jnp.zeros((SUB, LANES), jnp.float32)
    for u in range(NSRC // 8):
        found = tiles_of(u, [b * FOUR + STEP * (m + 1) for b in range(2) for m in range(4)])
        for b in range(2):
            for m in range(4):
                keys = keys + jnp.where(sub == 2 * m + b, found[b * FOUR + STEP * (m + 1)], 0.0)
    key_vmem[...] = keys.astype(jnp.int32)
    copy = pltpu.make_async_copy(key_vmem, key_ref, sem)
    copy.start()
    for acc in accs:
        acc[...] = jnp.zeros_like(acc)
    copy.wait()

    @pl.loop(0, NSRC // 8)
    def _(u):
        found = tiles_of(u, range(2 * FOUR))
        for b in range(2):
            for m in range(4):
                for t in range(NT):
                    row = key_ref[2 * m + b, u * 8 + t] * SUB
                    where = pl.ds(pl.multiple_of(row, SUB), SUB)
                    for half in range(2):
                        first = b * FOUR + STEP * m
                        tile = found[first + 2 * t + half]
                        if t == 0 and half == 0 and m > 0:
                            tile = jnp.where(sub >= 2 * m, tile, found[first + STEP])
                        acc = accs[half * COPIES + (m + t) % COPIES]
                        acc[where, :] = acc[where, :] + tile

    core = lax.axis_index("c")
    for ref, parity in ((keep_ref, core), (send_ref, 1 - core)):
        for high in range(2):
            rows = pl.ds(pl.multiple_of((high * 2 + parity) * SITE_ROWS, SUB), SITE_ROWS)
            for half in range(2):
                total = accs[half * COPIES][rows, :]
                for other in range(1, COPIES):
                    total = total + accs[half * COPIES + other][rows, :]
                ref[high, half] = total.astype(ref.dtype)


def make_sums(arrived):
    shape = (2, 2, SITE_ROWS, LANES)
    return pl.pallas_call(
        sum_kernel,
        in_specs=[pl.BlockSpec(memory_space=pltpu.VMEM)],
        out_specs=[pl.BlockSpec(memory_space=pltpu.VMEM)] * 2,
        out_shape=[
            jax.ShapeDtypeStruct(shape, jnp.float32),
            jax.ShapeDtypeStruct(shape, jnp.bfloat16),
        ],
        scratch_shapes=[
            pltpu.VMEM((SUB, LANES), jnp.int32),
            pltpu.SMEM((SUB, LANES), jnp.int32),
            pltpu.SemaphoreType.DMA,
        ]
        + [pltpu.VMEM((BUCKETS * SUB, LANES), jnp.float32)] * (2 * COPIES),
        compiler_params=pltpu.CompilerParams(vmem_limit_bytes=32 * MIB),
        cost_estimate=pl.CostEstimate(
            flops=NSRC * NT * 2 * BLK, bytes_accessed=2 * MIB, transcendentals=0
        ),
        name="sums",
    )(arrived)


def join_kernel(keep_ref, both_ref, out_ref):
    got = both_ref[1 - lax.axis_index("c")].astype(jnp.float32)
    total = (keep_ref[...] + got).astype(jnp.bfloat16)
    for x in range(4):
        out_ref[x] = total


def make_join(keep, both):
    return pl.pallas_call(
        join_kernel,
        in_specs=[pl.BlockSpec(memory_space=pltpu.VMEM)] * 2,
        out_specs=pl.BlockSpec(memory_space=pltpu.VMEM),
        out_shape=jax.ShapeDtypeStruct((4, 2, 2, SITE_ROWS, LANES), jnp.bfloat16),
        compiler_params=pltpu.CompilerParams(vmem_limit_bytes=32 * MIB),
        name="join",
    )(keep, both)


HALF = LANES // 2
NHI = 32
KPAD = 16


def fit_kernel(in_ref, weight_ref, out_ref, scr):
    site = lax.axis_index("yl") * 2 + lax.axis_index("c")
    for k in range(NU_SITE):
        rows = [
            jnp.concatenate([in_ref[x, q, pl.ds(k * SUB, SUB), :] for q in range(4)], axis=0)
            for x in range(4)
        ]
        low = jnp.concatenate([r[:, :HALF] for r in rows], axis=1)
        high = jnp.concatenate([r[:, HALF:] for r in rows], axis=1)
        res = lax.dot_general(
            jnp.concatenate([low, high], axis=0),
            weight_ref[site * NU_SITE + k],
            (((1,), (1,)), ((), ())),
            preferred_element_type=jnp.float32,
        )
        scr[pl.ds(k, NHI, stride=KPAD), :] = jnp.concatenate([res[:NHI], res[NHI:]], axis=1)
    for n in range(NHI):
        out_ref[:, n * LANES : (n + 1) * LANES] = scr[n * KPAD : n * KPAD + NU_SITE, :].astype(
            jnp.bfloat16
        )


def make_fit(gathered, fitting):
    return pl.pallas_call(
        fit_kernel,
        in_specs=[pl.BlockSpec(memory_space=pltpu.VMEM)] * 2,
        out_specs=pl.BlockSpec(memory_space=pltpu.VMEM),
        out_shape=jax.ShapeDtypeStruct((NU_SITE, NHI * LANES), jnp.bfloat16),
        scratch_shapes=[pltpu.VMEM((NHI * KPAD, LANES), jnp.float32)],
        compiler_params=pltpu.CompilerParams(vmem_limit_bytes=32 * MIB),
        name="fit",
    )(gathered, fitting)


def local(three_center, pair_mu, pair_site, pair_pos, coeff, fitting):
    pieces = make_pieces(three_center, pair_mu, pair_site, pair_pos, coeff)
    arrived = lax.all_to_all(
        pieces.reshape(NSRC, UNIT // 2, 2, LANES), MAIN, split_axis=0, concat_axis=0, tiled=True
    )
    keep, send = make_sums(arrived.reshape(NSRC * UNIT, LANES))
    both = lax.all_gather(send, "c", axis=0)
    sums = make_join(keep, both)
    gathered = lax.all_to_all(
        sums.reshape(8, 2 * SITE_ROWS, LANES), FIT, split_axis=0, concat_axis=0, tiled=True
    )
    result = make_fit(gathered.reshape(4, 4, NU_SITE * SUB, LANES), fitting)
    return result.reshape(1, NU_SITE, 1, 4096)


def solution(mesh):
    fine = Mesh(mesh.devices.reshape(8, 4, 2, 2, 4), ("z", "yh", "yl", "c", "x"))
    mu = ("z", "yh", "yl", "c")
    in_specs = (
        P(mu, None, "x"),
        P(mu, None),
        P(mu, None, None),
        P(mu, None),
        P(),
        P(None, "x", None),
    )
    out_specs = P(mu, None, None, "x")
    return jax.shard_map(local, mesh=fine, in_specs=in_specs, out_specs=out_specs, check_vma=False)
```
